32 devices in a mesh: seq: 8 (over z, y), rep: 4 (over x, core).
Axes of the slice: x: 2, y: 2, z: 4, core: 2. Of those that a mesh axis runs over, the one named last changes fastest.
Arguments:
- atom_single: bfloat16 [65536, 128], P(('seq', 'rep')), may hold values from -6 to 6
- token_single: bfloat16 [8192, 384], P('seq'), may hold values from -6 to 6
- tok_weight: bfloat16 [384, 128], replicated, may hold values from -0.3125 to 0.3125
- atom_gain: float32 [128], replicated, may hold values from 0.1 to 1.9
- w_query: bfloat16 [128, 128], replicated, may hold values from -0.5 to 0.5
- w_key: bfloat16 [128, 128], replicated, may hold values from -0.5 to 0.5
- w_value: bfloat16 [128, 128], replicated, may hold values from -0.5 to 0.5
- pair_weight: float32 [16, 4], replicated, may hold values from -1.5 to 1.5
- out_weight: bfloat16 [128, 128], replicated, may hold values from -0.5 to 0.5
- pair_feats: bfloat16 [65536, 16, 128], P(('seq', 'rep')), may hold values from -110 to 110
- counts: int32 [8192], P('seq'), may hold values from 1 to 15, as said below
- atom_token: int32 [65536], P(('seq', 'rep')), may hold values from 0 to 8191, as said below
- window_shift: int32 [2048], P(('seq', 'rep')), may hold values from 0 to 96
- atom_cot: bfloat16 [65536, 128], P(('seq', 'rep')), may hold values from -6 to 6
Outputs:
- atom_out: bfloat16 [65536, 128], P(('seq', 'rep'))
- token_mean: bfloat16 [8192, 128], P('seq')
- atom_grad: bfloat16 [65536, 128], P(('seq', 'rep'))
- token_grad: bfloat16 [8192, 384], P('seq')
The draws below stay inside these ranges and needn't reach their ends.
Inputs may be any that keep to these rules, and one draw needn't show every extreme that they name: The counts sum to 65536; the atoms held by one index of seq belong to tokens of that index or to at most 512 tokens just below its token range, never to tokens above it. `atom_token`: token t owns the counts[t] atoms that follow the atoms of tokens 0 to t - 1, in order.
All inputs are finite; a program needn't handle non-finite values.
Results may differ from the reference program's by a relative error of at most 0.009.
Values may be sent and summed in bfloat16 or wider, within the bound.
No kernel may reach another device: no remote copies, remote signals or barrier semaphores. Data moves between devices by JAX's collectives and lax.ppermute only.
A program may use at most 128 MiB of HBM per device.

```python
import math
import jax
import jax.numpy as jnp
from jax import lax

ATOM_W = 128
TOK_W = 384
HEADS = 4
PAIR_W = 16
QUERY_BLOCK = 32
KEY_SPAN = 128
REACH = 96
TOK_DEV = 1024
ATOMS = 65536
TOKENS = 8192
WINDOWS = 2048
N_SEQ = 8


def mirrored(rng_keys, offsets):

    def flipped(one_key, row):
        return -jax.random.permutation(one_key, row)
    return jnp.concatenate([offsets, jax.vmap(flipped)(rng_keys, offsets)], axis=1)


def token_counts(key):
    half_rows = TOK_DEV // 2
    quarter_rows = TOK_DEV // 4
    key_slope, key_end, key_perm = jax.random.split(key, 3)
    narrow = jax.random.randint(key_slope, (N_SEQ - 1, half_rows), -1, 2)
    places = jnp.arange(N_SEQ, dtype=jnp.int32)
    target = jnp.where((places % 2 == 1) | (places == N_SEQ - 2), 1, 0)
    target = target.at[0].set(0).at[N_SEQ - 1].set(0)
    climb = (target[1:] - target[:-1])[:, None]
    border = jax.random.randint(key_end, (2, quarter_rows), -7, 8)
    border = border.at[0, 0].set(7)
    perm_keys = jax.random.split(key_perm, N_SEQ + 1)
    middle_counts = (8 + 2 * climb + mirrored(perm_keys[:N_SEQ - 1], narrow)).reshape(-1)
    border_counts = 8 + mirrored(perm_keys[N_SEQ - 1:], border)
    return jnp.concatenate([border_counts[0], middle_counts, border_counts[1]]).astype(jnp.int32)


def draw_counts(key, part):
    shared = token_counts(key)
    return shared


def draw_atom_token(key, part):
    shared = token_counts(key)
    return jnp.repeat(jnp.arange(TOKENS, dtype=jnp.int32), shared, total_repeat_length=ATOMS)


def draw_window_shift(key, part):
    key = jax.random.fold_in(key, 5)
    shifts = jax.random.randint(key, (WINDOWS,), 0, REACH + 1)
    return shifts.at[0].set(0).at[1].set(REACH).astype(jnp.int32)


def draw_pair_feats(key, part):
    key = jax.random.fold_in(key, 7)
    key_base = jax.random.fold_in(key, 0)
    shape = (ATOMS, PAIR_W, KEY_SPAN)
    values = jnp.clip(jax.random.normal(key_base, shape, jnp.float32), -6.0, 6.0)
    return values.astype(jnp.bfloat16)


def shard_levels(rng, dims, cuts, least, top_value):
    def one(dim, blocks):
        steps = jax.random.uniform(jax.random.fold_in(jax.random.fold_in(rng, 6), dim), (blocks,), jnp.float32, least / len(cuts), top_value / len(cuts))
        return jnp.repeat(jnp.exp(steps), dims[dim] // blocks).reshape((-1,) + (1,) * (len(dims) - dim - 1))

    factor_of = one(*cuts[0])
    for cut in cuts[1:]:
        factor_of = factor_of * one(*cut)
    return factor_of


def gaussian(own_key, shape, scale, limit, shards=(), held_as=jnp.bfloat16):
    drawn = scale * jax.random.normal(own_key, shape, jnp.float32)
    if shards:
        drawn = drawn * shard_levels(own_key, shape, shards, -0.22, 0.18)
    return jnp.clip(drawn, -limit, limit).astype(held_as)


def setup_inputs(seed: int = 0) -> dict:
    streams_of = jax.random.split(jax.random.key(seed), 15)
    atom_single = gaussian(streams_of[0], (ATOMS, ATOM_W), 1.0, 6.0, ((0, 32),))
    token_single = gaussian(streams_of[1], (TOKENS, TOK_W), 1.0, 6.0, ((0, 8),))
    tok_weight = gaussian(streams_of[2], (TOK_W, ATOM_W), TOK_W ** -0.5, 0.3125)
    atom_gain = jnp.clip(1.0 + 0.18 * jax.random.normal(streams_of[3], (ATOM_W,), jnp.float32), 0.1, 1.9)
    w_query = gaussian(streams_of[4], (ATOM_W, ATOM_W), ATOM_W ** -0.5, 0.5)
    w_key = gaussian(streams_of[5], (ATOM_W, ATOM_W), ATOM_W ** -0.5, 0.5)
    w_value = gaussian(streams_of[6], (ATOM_W, ATOM_W), ATOM_W ** -0.5, 0.5)
    pair_weight = gaussian(streams_of[7], (PAIR_W, HEADS), PAIR_W ** -0.5, 1.5, (), jnp.float32)
    out_weight = gaussian(streams_of[8], (ATOM_W, ATOM_W), ATOM_W ** -0.5, 0.5)
    pair_feats = draw_pair_feats(jax.random.fold_in(streams_of[14], 71), 0)
    counts = draw_counts(jax.random.fold_in(streams_of[14], 71), 0)
    atom_token = draw_atom_token(jax.random.fold_in(streams_of[14], 71), 0)
    window_shift = draw_window_shift(jax.random.fold_in(streams_of[14], 71), 0)
    atom_cot = gaussian(streams_of[13], (ATOMS, ATOM_W), 1.0, 6.0, ((0, 32),))
    return {"atom_single": atom_single, "token_single": token_single, "tok_weight": tok_weight, "atom_gain": atom_gain, "w_query": w_query, "w_key": w_key, "w_value": w_value, "pair_weight": pair_weight, "out_weight": out_weight, "pair_feats": pair_feats, "counts": counts, "atom_token": atom_token, "window_shift": window_shift, "atom_cot": atom_cot}


HIGHEST = lax.Precision.HIGHEST

def rounded(values):
    lowered = lax.optimization_barrier(lax.stop_gradient(values).astype(jnp.bfloat16))
    return values + (lowered.astype(jnp.float32) - lax.stop_gradient(values))

def product(left, right):
    return jnp.dot(left, right, precision=HIGHEST, preferred_element_type=jnp.float32)

def normalize(hidden, atom_gain):
    center = hidden - lax.optimization_barrier(jnp.mean(hidden, axis=-1, keepdims=True))
    spread = lax.optimization_barrier(jnp.mean(center * center, axis=-1, keepdims=True))
    return center * lax.rsqrt(spread + 1e-05) * atom_gain.astype(jnp.float32)

def front(hidden, atom_gain, w_query, w_key, w_value):
    normed = rounded(normalize(hidden, atom_gain))
    query = rounded(product(normed, w_query.astype(jnp.float32)))
    keys = rounded(product(normed, w_key.astype(jnp.float32)))
    values = rounded(product(normed, w_value.astype(jnp.float32)))
    return (query, jnp.concatenate([keys, values], axis=1))

def attend_windows(query_rows, kv_keys, pair_rows, pair_weight, valid):
    nwin, qrows, width = query_rows.shape
    head_size = width // HEADS
    query = query_rows.reshape(nwin, qrows, HEADS, head_size)
    keys = kv_keys[:, :, :width].reshape(nwin, -1, HEADS, head_size)
    values = kv_keys[:, :, width:].reshape(nwin, -1, HEADS, head_size)
    bias = jnp.einsum('bqck,ch->bqhk', pair_rows.astype(jnp.float32), pair_weight.astype(jnp.float32), precision=HIGHEST)
    scores = jnp.einsum('bqhd,bkhd->bqhk', query, keys, precision=HIGHEST) * head_size ** (-0.5) + bias
    scores = jnp.where(valid[:, None, None, :], scores, -1e+30)
    row_max = lax.stop_gradient(lax.optimization_barrier(jnp.max(scores, axis=-1, keepdims=True)))
    weights = jnp.exp(scores - row_max)
    probs = rounded(weights / lax.optimization_barrier(jnp.sum(weights, axis=-1, keepdims=True)))
    mixed = jnp.einsum('bqhk,bkhd->bqhd', probs, values, precision=HIGHEST)
    return rounded(mixed.reshape(nwin, qrows, width))

def block_forward(atom_f, token_f, atom_token, tok_weight, atom_gain, w_query, w_key, w_value, pair_weight, out_weight, pair_feats, window_shift):
    tok_proj = rounded(product(token_f, tok_weight.astype(jnp.float32)))
    hidden = atom_f + tok_proj[atom_token]
    query, key_values = front(hidden, atom_gain, w_query, w_key, w_value)
    total_atoms = hidden.shape[0]
    starts = QUERY_BLOCK * jnp.arange(WINDOWS, dtype=jnp.int32) - REACH + window_shift
    positions = starts[:, None] + jnp.arange(KEY_SPAN, dtype=jnp.int32)[None, :]
    valid = (positions >= 0) & (positions < total_atoms)
    index_rows = jnp.clip(positions, 0, total_atoms - 1).astype(jnp.int32)
    per_group = math.gcd(WINDOWS, 64)
    groups = WINDOWS // per_group

    def one_group(pieces):
        query_block, index_block, valid_block, pair_block = pieces
        return attend_windows(query_block, key_values[index_block], pair_block, pair_weight, valid_block)
    outputs = lax.map(one_group, (query.reshape(groups, per_group, QUERY_BLOCK, ATOM_W), index_rows.reshape(groups, per_group, KEY_SPAN), valid.reshape(groups, per_group, KEY_SPAN), pair_feats.reshape(groups, per_group, QUERY_BLOCK, PAIR_W, KEY_SPAN)))
    attn = outputs.reshape(total_atoms, ATOM_W)
    return hidden + product(attn, out_weight.astype(jnp.float32))

def reference(atom_single, token_single, tok_weight, atom_gain, w_query, w_key, w_value, pair_weight, out_weight, pair_feats, counts, atom_token, window_shift, atom_cot):

    def run_block(atom_f, token_f):
        return block_forward(atom_f, token_f, atom_token, tok_weight, atom_gain, w_query, w_key, w_value, pair_weight, out_weight, pair_feats, window_shift)
    result, pullback = jax.vjp(run_block, atom_single.astype(jnp.float32), token_single.astype(jnp.float32))
    atom_grad, token_grad = pullback(atom_cot.astype(jnp.float32))
    atom_out = result.astype(jnp.bfloat16)
    totals = jax.ops.segment_sum(atom_out.astype(jnp.float32), atom_token, num_segments=TOKENS)
    token_mean = (totals / counts.astype(jnp.float32)[:, None]).astype(jnp.bfloat16)
    return (atom_out, token_mean, atom_grad.astype(jnp.bfloat16), token_grad.astype(jnp.bfloat16))
```

```python
import functools

import jax
import jax.numpy as jnp
from jax import lax
from jax.experimental import pallas as pl
from jax.experimental.pallas import tpu as pltpu
from jax.sharding import PartitionSpec as P

HEADS = 4
QUERY_BLOCK = 32
KEY_SPAN = 128
REACH = KEY_SPAN - QUERY_BLOCK
HALF = QUERY_BLOCK // 2
SUB = 128
SPAN = 256
STEP_WINDOWS = 4
BF = jnp.bfloat16
F32 = jnp.float32
MIB = 1 << 20


def dot(left, right):
    return jnp.dot(left, right, preferred_element_type=F32)


def dot_nt(left, right):
    return lax.dot_general(left, right, (((1,), (1,)), ((), ())), preferred_element_type=F32)


def dot_tn(left, right):
    return lax.dot_general(left, right, (((0,), (0,)), ((), ())), preferred_element_type=F32)


def whole(shape):
    return pl.BlockSpec(shape, lambda *_: (0,) * len(shape))


def row_block(rows, width):
    return pl.BlockSpec((rows, width), lambda i: (i, 0))


def token_base(tok_smem, block, offset, tok_ext):
    first = tok_smem[block, 0] - offset
    first = jnp.clip(first, 0, tok_ext - 1)
    return pl.multiple_of(first // 16 * 16, 16)


def front_kernel(
    tok_smem, place, atom, tok, below, proj, gain, w_front, hidden_out, query_out, kv_out, table
):
    step = pl.program_id(0)
    half = below.shape[0]
    own = proj.shape[0]

    @pl.when(step == 0)
    def _():
        table[0:half, :] = below[...]
        table[half : half + own, :] = proj[...]
        table[half + own :, :] = jnp.zeros((SPAN, table.shape[1]), BF)

    blocks = atom.shape[0] // SUB
    width = atom.shape[1]
    lane = lax.broadcasted_iota(jnp.int32, (SUB, SPAN), 1).astype(F32)
    for k in range(blocks):
        block = step * blocks + k
        base = token_base(tok_smem, block, place[0], half + own)
        ids = (tok[pl.ds(block, 1), :] - (place[0] + base)).astype(F32)
        ids = jnp.broadcast_to(ids, (SUB, SUB)).T
        ids = jnp.concatenate([ids, ids], axis=1)
        one_hot = jnp.where(ids == lane, 1.0, 0.0).astype(BF)
        rows = pl.ds(k * SUB, SUB)
        hidden = atom[rows, :].astype(F32) + dot(one_hot, table[pl.ds(base, SPAN), :])
        hidden_out[rows, :] = hidden
        center = hidden - jnp.mean(hidden, axis=-1, keepdims=True)
        spread = jnp.mean(center * center, axis=-1, keepdims=True)
        normed = (center * lax.rsqrt(spread + 1e-05) * gain[...]).astype(BF)
        projected = dot(normed, w_front[...]).astype(BF)
        query_out[rows, :] = projected[:, :width]
        kv_out[rows, :] = projected[:, width:]


def window_kernel(
    shift_smem,
    place,
    kv,
    kv_low,
    kv_high,
    query,
    hidden,
    cot,
    pair,
    bias_weight,
    out_weight,
    out_ref,
    dq_ref,
    dkv_ref,
    dlow_ref,
    dhigh_ref,
    keys_s,
    values_s,
    dkeys_s,
    dvalues_s,
):
    step = pl.program_id(0)
    atoms = kv.shape[0]
    width = query.shape[1]
    head = width // HEADS
    scale = head ** (-0.5)

    @pl.when(step == 0)
    def _():
        for target, cols in ((keys_s, slice(0, width)), (values_s, slice(width, 2 * width))):
            target[0:REACH, :] = kv_low[:, cols].astype(F32)
            target[REACH : REACH + atoms, :] = kv[:, cols].astype(F32)
            target[REACH + atoms :, :] = kv_high[:, cols].astype(F32)
        dkeys_s[...] = jnp.zeros_like(dkeys_s)
        dvalues_s[...] = jnp.zeros_like(dvalues_s)

    lane = lax.broadcasted_iota(jnp.int32, (HALF, width), 1) // head
    d_attn = dot_nt(cot[...], out_weight[...]).astype(BF)
    key_lane = lax.broadcasted_iota(jnp.int32, (1, KEY_SPAN), 1)

    def stacked(rows):
        parts = []
        for half in range(2):
            piece = rows[half * HALF : (half + 1) * HALF, :]
            for h in range(HEADS):
                parts.append(jnp.where(lane == h, piece, jnp.zeros_like(piece)))
        return jnp.concatenate(parts, axis=0)

    def unstacked(rows):
        parts = []
        for half in range(2):
            piece = None
            for h in range(HEADS):
                at = (half * HEADS + h) * HALF
                part = rows[at : at + HALF, :]
                piece = part if piece is None else jnp.where(lane == h, part, piece)
            parts.append(piece)
        return jnp.concatenate(parts, axis=0)

    attn_parts, d_keys, d_values, starts = [], [], [], []
    for k in range(STEP_WINDOWS):
        window = step * STEP_WINDOWS + k
        start = window * QUERY_BLOCK + shift_smem[window]
        starts.append(start)
        first = place[0] + start
        ok = (key_lane + first >= 0) & (key_lane + first < place[1])
        keys = keys_s[pl.ds(start, KEY_SPAN), :].astype(BF)
        values = values_s[pl.ds(start, KEY_SPAN), :].astype(BF)
        q_rows = stacked(query[k * QUERY_BLOCK : (k + 1) * QUERY_BLOCK, :])
        g_rows = stacked(d_attn[k * QUERY_BLOCK : (k + 1) * QUERY_BLOCK, :])
        feats = pair.shape[0] // (STEP_WINDOWS * 2)
        both = jnp.concatenate(
            [
                pair[(2 * k) * feats : (2 * k + 1) * feats, :],
                pair[(2 * k + 1) * feats : (2 * k + 2) * feats, :],
            ],
            axis=1,
        )
        parts = dot(bias_weight[...], both)
        third = HEADS * HALF
        bias = parts[:third] + (parts[third : 2 * third] + parts[2 * third :])
        bias = jnp.concatenate([bias[:, :KEY_SPAN], bias[:, KEY_SPAN:]], axis=0)
        scores = jnp.where(ok, dot_nt(q_rows, keys) * scale + bias, -1e30)
        weights = jnp.exp(scores - jnp.max(scores, axis=-1, keepdims=True))
        probs = weights * (1.0 / jnp.sum(weights, axis=-1, keepdims=True))
        probs_bf = probs.astype(BF)
        attn_parts.append(unstacked(dot(probs_bf, values)))
        d_probs = dot_nt(g_rows, values)
        d_scores = probs * (d_probs - jnp.sum(probs * d_probs, axis=-1, keepdims=True))
        d_scores = (d_scores * scale).astype(BF)
        d_values.append(dot_tn(probs_bf, g_rows))
        d_keys.append(dot_tn(d_scores, q_rows))
        dq_ref[k * QUERY_BLOCK : (k + 1) * QUERY_BLOCK, :] = unstacked(
            dot(d_scores, keys)
        ).astype(BF)
    for k in range(STEP_WINDOWS):
        dkeys_s[pl.ds(starts[k], KEY_SPAN), :] += d_keys[k]
        dvalues_s[pl.ds(starts[k], KEY_SPAN), :] += d_values[k]
    attn = jnp.concatenate(attn_parts, axis=0).astype(BF)
    out_ref[...] = (hidden[...] + dot(attn, out_weight[...])).astype(BF)

    @pl.when(step == pl.num_programs(0) - 1)
    def _():
        for source, cols in ((dkeys_s, slice(0, width)), (dvalues_s, slice(width, 2 * width))):
            dlow_ref[:, cols] = source[0:REACH, :].astype(BF)
            dkv_ref[:, cols] = source[REACH : REACH + atoms, :].astype(BF)
            dhigh_ref[:, cols] = source[REACH + atoms :, :].astype(BF)


def back_kernel(
    tok_smem,
    place,
    tok,
    cot,
    hidden,
    out,
    dq,
    dkv,
    rim_low,
    rim_high,
    gain,
    w_front,
    grad_ref,
    sums_ref,
    total_s,
):
    step = pl.program_id(0)
    last = pl.num_programs(0) - 1
    rows_in = cot.shape[0]
    width = cot.shape[1]
    tok_ext = total_s.shape[0] - SPAN

    @pl.when(step == 0)
    def _():
        total_s[...] = jnp.zeros_like(total_s)

    d_kv = dkv[...].astype(F32)
    low = jnp.where(step == 0, rim_low[...].astype(F32), 0.0)
    high = jnp.where(step == last, rim_high[...].astype(F32), 0.0)
    d_kv = jnp.concatenate(
        [d_kv[:REACH] + low, d_kv[REACH : rows_in - REACH], d_kv[rows_in - REACH :] + high], axis=0
    )
    d_projected = jnp.concatenate([dq[...], d_kv.astype(BF)], axis=1)
    d_normed = dot_nt(d_projected, w_front[...])
    h = hidden[...]
    center = h - jnp.mean(h, axis=-1, keepdims=True)
    spread = jnp.mean(center * center, axis=-1, keepdims=True)
    inv = lax.rsqrt(spread + 1e-05)
    unit = center * inv
    g = d_normed * gain[...]
    d_front = inv * (
        g
        - jnp.mean(g, axis=-1, keepdims=True)
        - unit * jnp.mean(g * unit, axis=-1, keepdims=True)
    )
    grad = (cot[...].astype(F32) + d_front).astype(BF)
    grad_ref[...] = grad
    both = jnp.concatenate([grad, out[...]], axis=1)
    row = lax.broadcasted_iota(jnp.int32, (SPAN, SUB), 0)
    blocks = rows_in // SUB
    for k in range(blocks):
        block = step * blocks + k
        base = token_base(tok_smem, block, place[0], tok_ext)
        ids = tok[pl.ds(block, 1), :] - (place[0] + base)
        one_hot = jnp.where(row == ids, 1.0, 0.0).astype(BF)
        total_s[pl.ds(base, SPAN), :] += dot(one_hot, both[k * SUB : (k + 1) * SUB, :])

    @pl.when(step == last)
    def _():
        quarter = tok_ext // 6
        for c in range(2):
            for k in range(3):
                at = (2 * k + c) * quarter
                sums_ref[c, k * quarter : (k + 1) * quarter, :] = total_s[
                    at : at + quarter, :
                ].astype(BF)


def split_parts(values, pieces):
    parts = []
    remainder = values
    for _ in range(pieces):
        upper = remainder.astype(BF)
        parts.append(upper)
        remainder = remainder - upper.astype(F32)
    return parts


def bias_matrix(pair_weight):
    parts = jnp.stack(split_parts(pair_weight, 3))
    eye = jnp.eye(HALF, dtype=BF)
    full = parts.transpose(0, 2, 1)[:, :, None, None, :] * eye[None, None, :, :, None]
    return full.reshape(3 * HEADS * HALF, HALF * pair_weight.shape[0])


def body(
    atom_single,
    token_single,
    tok_weight,
    atom_gain,
    w_query,
    w_key,
    w_value,
    pair_weight,
    out_weight,
    pair_feats,
    counts,
    atom_token,
    window_shift,
    atom_cot,
):
    seq = lax.axis_size("seq")
    rep = lax.axis_size("rep")
    seq_place = lax.axis_index("seq")
    rep_place = lax.axis_index("rep")
    group_place = seq_place * rep + rep_place
    atoms, width = atom_single.shape
    tok_rows = token_single.shape[0]
    half_rows = tok_rows // 2
    total_atoms = atoms * seq * rep
    smem = pl.BlockSpec(memory_space=pltpu.SMEM)

    proj = dot(token_single, tok_weight).astype(BF)
    below = lax.ppermute(proj[tok_rows - half_rows :], "seq", [(i, i + 1) for i in range(seq - 1)])
    tok_place = (seq_place * tok_rows - half_rows).reshape(1)
    tok2 = atom_token.reshape(atoms // SUB, SUB)
    gain = atom_gain.reshape(1, width)
    w_front = jnp.concatenate([w_query, w_key, w_value], axis=1)
    rows = 256
    hidden, query, key_values = pl.pallas_call(
        front_kernel,
        grid=(atoms // rows,),
        in_specs=[
            smem,
            smem,
            row_block(rows, width),
            whole(tok2.shape),
            whole(below.shape),
            whole(proj.shape),
            whole(gain.shape),
            whole(w_front.shape),
        ],
        out_specs=[row_block(rows, width), row_block(rows, width), row_block(rows, 2 * width)],
        out_shape=[
            jax.ShapeDtypeStruct((atoms, width), F32),
            jax.ShapeDtypeStruct((atoms, width), BF),
            jax.ShapeDtypeStruct((atoms, 2 * width), BF),
        ],
        scratch_shapes=[pltpu.VMEM((half_rows + tok_rows + SPAN, width), BF)],
        compiler_params=pltpu.CompilerParams(vmem_limit_bytes=48 * MIB),
        name="front",
    )(tok2, tok_place, atom_single, tok2, below, proj, gain, w_front)

    count = seq * rep
    up = [(i, i + 1) for i in range(count - 1)]
    down = [(i + 1, i) for i in range(count - 1)]
    axes = ("seq", "rep")
    kv_low = lax.ppermute(key_values[atoms - REACH :], axes, up)
    kv_high = lax.ppermute(key_values[:REACH], axes, down)

    windows = atoms // QUERY_BLOCK
    step_rows = STEP_WINDOWS * QUERY_BLOCK
    channels = pair_feats.shape[1]
    pair2 = pair_feats.reshape(atoms * channels, KEY_SPAN)
    bias_weight = bias_matrix(pair_weight)
    win_place = jnp.stack([group_place * atoms - REACH, jnp.int32(total_atoms)])
    scratch = pltpu.VMEM((atoms + 2 * REACH, width), F32)
    atom_out, d_query, d_kv, d_low, d_high = pl.pallas_call(
        window_kernel,
        grid=(windows // STEP_WINDOWS,),
        in_specs=[
            smem,
            smem,
            whole(key_values.shape),
            whole(kv_low.shape),
            whole(kv_high.shape),
            row_block(step_rows, width),
            row_block(step_rows, width),
            row_block(step_rows, width),
            row_block(step_rows * channels, KEY_SPAN),
            whole(bias_weight.shape),
            whole(out_weight.shape),
        ],
        out_specs=[
            row_block(step_rows, width),
            row_block(step_rows, width),
            whole(key_values.shape),
            whole(kv_low.shape),
            whole(kv_high.shape),
        ],
        out_shape=[
            jax.ShapeDtypeStruct((atoms, width), BF),
            jax.ShapeDtypeStruct((atoms, width), BF),
            jax.ShapeDtypeStruct((atoms, 2 * width), BF),
            jax.ShapeDtypeStruct((REACH, 2 * width), BF),
            jax.ShapeDtypeStruct((REACH, 2 * width), BF),
        ],
        scratch_shapes=[scratch] * 4,
        compiler_params=pltpu.CompilerParams(vmem_limit_bytes=48 * MIB),
        name="windows",
    )(
        window_shift,
        win_place,
        key_values,
        kv_low,
        kv_high,
        query,
        hidden,
        atom_cot,
        pair2,
        bias_weight,
        out_weight,
    )

    rim_high = lax.ppermute(d_low, axes, down)
    rim_low = lax.ppermute(d_high, axes, up)
    tok_ext = half_rows + tok_rows
    atom_grad, sums = pl.pallas_call(
        back_kernel,
        grid=(atoms // rows,),
        in_specs=[
            smem,
            smem,
            whole(tok2.shape),
            row_block(rows, width),
            row_block(rows, width),
            row_block(rows, width),
            row_block(rows, width),
            row_block(rows, 2 * width),
            whole(rim_low.shape),
            whole(rim_high.shape),
            whole(gain.shape),
            whole(w_front.shape),
        ],
        out_specs=[row_block(rows, width), whole((2, tok_ext // 2, 2 * width))],
        out_shape=[
            jax.ShapeDtypeStruct((atoms, width), BF),
            jax.ShapeDtypeStruct((2, tok_ext // 2, 2 * width), BF),
        ],
        scratch_shapes=[pltpu.VMEM((tok_ext + SPAN, 2 * width), F32)],
        compiler_params=pltpu.CompilerParams(vmem_limit_bytes=48 * MIB),
        name="back",
    )(tok2, tok_place, tok2, atom_cot, hidden, atom_out, d_query, d_kv, rim_low, rim_high, gain, w_front)

    core = rep_place % 2
    quarter = tok_ext // 6
    mine = lax.dynamic_index_in_dim(sums, core, 0, keepdims=False)
    other = lax.dynamic_index_in_dim(sums, 1 - core, 0, keepdims=False)
    swap = [(i, i ^ 1) for i in range(rep)]
    across = [(i, i ^ 2) for i in range(rep)]
    pair_sum = (mine.astype(F32) + lax.ppermute(other, "rep", swap).astype(F32)).astype(BF)
    low_part, own_part = pair_sum[:quarter], pair_sum[quarter:]
    straight = [(i, i - 1) for i in range(1, seq)]
    crossed = [((s + 1) * rep + r, s * rep + (r ^ 2)) for s in range(seq - 1) for r in range(rep)]
    got_own = lax.ppermute(own_part, "rep", across)
    got_straight = lax.ppermute(low_part, "seq", straight)
    got_crossed = lax.ppermute(low_part, axes, crossed)
    half_sum = own_part.astype(F32) + got_own.astype(F32)
    upper = half_sum[quarter:] + (got_straight.astype(F32) + got_crossed.astype(F32))
    half_sum = jnp.concatenate([half_sum[:quarter], upper], axis=0).astype(BF)
    other_sum = lax.ppermute(half_sum, "rep", swap)
    first = jnp.where(core == 0, half_sum, other_sum)
    second = jnp.where(core == 0, other_sum, half_sum)
    totals = jnp.concatenate(
        [first[:quarter], second[:quarter], first[quarter:], second[quarter:]], axis=0
    )
    token_grad = dot_nt(totals[:, :width], tok_weight).astype(BF)
    token_mean = (totals[:, width:].astype(F32) / counts.astype(F32)[:, None]).astype(BF)
    return (atom_out, token_mean, atom_grad, token_grad)


def solution(mesh):
    return jax.shard_map(
        body,
        mesh=mesh,
        in_specs=(
            P(("seq", "rep"), None),
            P("seq", None),
            P(),
            P(),
            P(),
            P(),
            P(),
            P(),
            P(),
            P(("seq", "rep"), None, None),
            P("seq"),
            P(("seq", "rep")),
            P(("seq", "rep")),
            P(("seq", "rep"), None),
        ),
        out_specs=(
            P(("seq", "rep"), None),
            P("seq", None),
            P(("seq", "rep"), None),
            P("seq", None),
        ),
        check_vma=False,
    )
```

```python
import jax
import jax.numpy as jnp
from jax import lax
from jax.experimental import pallas as pl
from jax.experimental.pallas import tpu as pltpu
from jax.sharding import PartitionSpec as P

HEADS = 4
QUERY_BLOCK = 32
KEY_SPAN = 128
REACH = KEY_SPAN - QUERY_BLOCK
HALF = QUERY_BLOCK // 2
SUB = 128
SPAN = 256
STEP_WINDOWS = 16
BIAS_PARTS = 2
BF = jnp.bfloat16
F32 = jnp.float32
VMEM = 60 << 20


def dot(left, right):
    return jnp.dot(left, right, preferred_element_type=F32)


def dot_nt(left, right):
    return lax.dot_general(left, right, (((1,), (1,)), ((), ())), preferred_element_type=F32)


def dot_tn(left, right):
    return lax.dot_general(left, right, (((0,), (0,)), ((), ())), preferred_element_type=F32)


def whole(shape):
    return pl.BlockSpec(shape, lambda *_: (0,) * len(shape))


def row_block(rows, width):
    return pl.BlockSpec((rows, width), lambda i: (i, 0))


def token_base(tok_smem, block, offset, tok_ext):
    first = tok_smem[block, 0] - offset
    first = jnp.clip(first, 0, tok_ext - 1)
    return pl.multiple_of(first // 16 * 16, 16)


def front_kernel(
    tok_smem,
    place,
    atom,
    tok,
    below,
    proj,
    gain,
    w_query,
    w_key,
    w_value,
    hidden_out,
    query_out,
    kv_out,
    first_out,
    last_out,
    table,
):
    step = pl.program_id(0)
    half = below.shape[0]
    own = proj.shape[0]
    rows_in, width = atom.shape

    @pl.when(step == 0)
    def _():
        table[0:half, :] = below[...]
        table[half : half + own, :] = proj[...]
        table[half + own :, :] = jnp.zeros((SPAN, width), BF)

    blocks = range(rows_in // SUB)
    lane = lax.broadcasted_iota(jnp.int32, (SUB, SPAN), 1).astype(F32)
    bases = [
        token_base(tok_smem, step * len(blocks) + k, place[0], half + own) for k in blocks
    ]
    ids = [tok[pl.ds(step * len(blocks) + k, 1), :] - (place[0] + bases[k]) for k in blocks]
    ids = [jnp.broadcast_to(row.astype(F32), (SUB, SUB)).T for row in ids]
    hot = [
        jnp.where(jnp.concatenate([row, row], axis=1) == lane, 1.0, 0.0).astype(BF) for row in ids
    ]
    token = [dot(hot[k], table[pl.ds(bases[k], SPAN), :]) for k in blocks]
    hidden = atom[...].astype(F32) + jnp.concatenate(token, axis=0)
    hidden_out[...] = hidden
    center = hidden - jnp.mean(hidden, axis=-1, keepdims=True)
    spread = jnp.mean(center * center, axis=-1, keepdims=True)
    normed = (center * lax.rsqrt(spread + 1e-05) * gain[...]).astype(BF)
    query_out[...] = dot(normed, w_query[...]).astype(BF)
    keys = dot(normed, w_key[...]).astype(BF)
    values = dot(normed, w_value[...]).astype(BF)
    both = jnp.concatenate([keys, values], axis=1)
    kv_out[...] = both

    @pl.when(step == 0)
    def _():
        first_out[...] = both[:REACH]

    @pl.when(step == pl.num_programs(0) - 1)
    def _():
        last_out[...] = both[rows_in - REACH :]


def window_kernel(
    shift_smem,
    place,
    kv,
    kv_low,
    kv_high,
    query,
    hidden,
    cot,
    pair,
    bias_weight,
    out_weight,
    out_ref,
    dq_ref,
    dkv_ref,
    dlow_ref,
    dhigh_ref,
    keys_s,
    values_s,
    dkeys_s,
    dvalues_s,
):
    step = pl.program_id(0)
    atoms = kv.shape[0]
    width = query.shape[1]
    head = width // HEADS
    scale = head ** (-0.5)

    @pl.when(step == 0)
    def _():
        for target, cols in ((keys_s, slice(0, width)), (values_s, slice(width, 2 * width))):
            target[0:REACH, :] = kv_low[:, cols].astype(F32)
            target[REACH : REACH + atoms, :] = kv[:, cols].astype(F32)
            target[REACH + atoms :, :] = kv_high[:, cols].astype(F32)
        dkeys_s[...] = jnp.zeros_like(dkeys_s)
        dvalues_s[...] = jnp.zeros_like(dvalues_s)

    lane = lax.broadcasted_iota(jnp.int32, (HALF, width), 1) // head
    key_lane = lax.broadcasted_iota(jnp.int32, (1, KEY_SPAN), 1)
    ones = jnp.ones((KEY_SPAN, KEY_SPAN), BF)
    count = query.shape[0] // QUERY_BLOCK
    feats = pair.shape[0] // (count * 2)
    heads = HEADS * HALF
    each = range(count)

    def stacked(rows):
        parts = []
        for half in range(2):
            piece = rows[half * HALF : (half + 1) * HALF, :]
            for h in range(HEADS):
                parts.append(jnp.where(lane == h, piece, jnp.zeros_like(piece)))
        return jnp.concatenate(parts, axis=0)

    def unstacked(rows):
        parts = []
        for half in range(2):
            piece = None
            for h in range(HEADS):
                at = (half * HEADS + h) * HALF
                part = rows[at : at + HALF, :]
                piece = part if piece is None else jnp.where(lane == h, part, piece)
            parts.append(piece)
        return jnp.concatenate(parts, axis=0)

    def pair_bias(k):
        at = 2 * k * feats
        both = jnp.concatenate(
            [pair[at : at + feats, :], pair[at + feats : at + 2 * feats, :]], axis=1
        )
        parts = dot(bias_weight[...], both)
        parts = parts[:heads] + parts[heads:]
        return jnp.concatenate([parts[:, :KEY_SPAN], parts[:, KEY_SPAN:]], axis=0)

    def block(k):
        return slice(k * QUERY_BLOCK, (k + 1) * QUERY_BLOCK)

    d_attn = dot_nt(cot[...], out_weight[...]).astype(BF)
    starts = [
        (step * count + k) * QUERY_BLOCK + shift_smem[step * count + k] for k in each
    ]
    spots = [key_lane + (place[0] + start) for start in starts]
    inside = [(spot >= 0) & (spot < place[1]) for spot in spots]
    keys = [keys_s[pl.ds(start, KEY_SPAN), :].astype(BF) for start in starts]
    values = [values_s[pl.ds(start, KEY_SPAN), :].astype(BF) for start in starts]
    q_rows = [stacked(query[block(k), :]) for k in each]
    g_rows = [stacked(d_attn[block(k), :]) for k in each]
    bias = [pair_bias(k) for k in each]
    scores = [
        jnp.where(inside[k], dot_nt(q_rows[k], keys[k]) * scale + bias[k], -1e30) for k in each
    ]
    weights = [jnp.exp(score - jnp.max(score, axis=-1, keepdims=True)) for score in scores]
    mixed = [
        dot(weights[k].astype(BF), jnp.concatenate([values[k], ones], axis=1)) for k in each
    ]
    inverse = [1.0 / rows[:, width:] for rows in mixed]
    probs = [weights[k] * inverse[k] for k in each]
    attn = [unstacked(mixed[k][:, :width] * inverse[k]) for k in each]
    d_probs = [dot_nt(g_rows[k], values[k]) for k in each]
    joint = [probs[k] * d_probs[k] for k in each]
    d_scores = [joint[k] - probs[k] * dot(joint[k].astype(BF), ones) for k in each]
    d_scores = [(rows * scale).astype(BF) for rows in d_scores]
    d_values = [dot_tn(probs[k].astype(BF), g_rows[k]) for k in each]
    d_keys = [dot_tn(d_scores[k], q_rows[k]) for k in each]
    for k in each:
        dq_ref[block(k), :] = unstacked(dot(d_scores[k], keys[k])).astype(BF)
    for k in each:
        dkeys_s[pl.ds(starts[k], KEY_SPAN), :] += d_keys[k]
        dvalues_s[pl.ds(starts[k], KEY_SPAN), :] += d_values[k]
    attn = jnp.concatenate(attn, axis=0).astype(BF)
    out_ref[...] = (hidden[...] + dot(attn, out_weight[...])).astype(BF)

    @pl.when(step == pl.num_programs(0) - 1)
    def _():
        for source, cols in ((dkeys_s, slice(0, width)), (dvalues_s, slice(width, 2 * width))):
            dlow_ref[:, cols] = source[0:REACH, :].astype(BF)
            dkv_ref[:, cols] = source[REACH : REACH + atoms, :].astype(BF)
            dhigh_ref[:, cols] = source[REACH + atoms :, :].astype(BF)


def back_kernel(
    tok_smem,
    place,
    tok,
    cot,
    hidden,
    out,
    dq,
    dkv,
    rim_low,
    rim_high,
    gain,
    w_query,
    w_key,
    w_value,
    grad_ref,
    mine_ref,
    other_ref,
    total_s,
):
    step = pl.program_id(0)
    last = pl.num_programs(0) - 1
    rows_in, width = cot.shape
    tok_ext = total_s.shape[0] - SPAN

    @pl.when(step == 0)
    def _():
        total_s[...] = jnp.zeros_like(total_s)

    low = jnp.where(step == 0, rim_low[...].astype(F32), 0.0)
    high = jnp.where(step == last, rim_high[...].astype(F32), 0.0)
    edge = rows_in - REACH
    d_kv = jnp.concatenate(
        [
            (dkv[:REACH, :].astype(F32) + low).astype(BF),
            dkv[REACH:edge, :],
            (dkv[edge:, :].astype(F32) + high).astype(BF),
        ],
        axis=0,
    )
    d_normed = dot_nt(dq[...], w_query[...])
    d_normed += dot_nt(d_kv[:, :width], w_key[...]) + dot_nt(d_kv[:, width:], w_value[...])
    rows = hidden[...]
    center = rows - jnp.mean(rows, axis=-1, keepdims=True)
    spread = jnp.mean(center * center, axis=-1, keepdims=True)
    inv = lax.rsqrt(spread + 1e-05)
    unit = center * inv
    scaled = d_normed * gain[...]
    d_front = inv * (
        scaled
        - jnp.mean(scaled, axis=-1, keepdims=True)
        - unit * jnp.mean(scaled * unit, axis=-1, keepdims=True)
    )
    grad = (cot[...].astype(F32) + d_front).astype(BF)
    grad_ref[...] = grad
    both = jnp.concatenate([grad, out[...]], axis=1)
    reach = SUB + 16
    row = lax.broadcasted_iota(jnp.int32, (reach, SUB), 0)
    blocks = range(rows_in // SUB)
    bases = [token_base(tok_smem, step * len(blocks) + k, place[0], tok_ext) for k in blocks]
    ids = [tok[pl.ds(step * len(blocks) + k, 1), :] - (place[0] + bases[k]) for k in blocks]
    hot = [jnp.where(row == line, 1.0, 0.0).astype(BF) for line in ids]
    sums = [dot(hot[k], both[k * SUB : (k + 1) * SUB, :]) for k in blocks]
    for k in blocks:
        total_s[pl.ds(bases[k], reach), :] += sums[k]

    @pl.when(step == last)
    def _():
        quarter = tok_ext // 6
        for target, core in ((mine_ref, place[1]), (other_ref, 1 - place[1])):
            for k in range(3):
                at = pl.multiple_of((2 * k + core) * quarter, quarter)
                target[k * quarter : (k + 1) * quarter, :] = total_s[pl.ds(at, quarter), :].astype(BF)


def split_parts(values, pieces):
    parts = []
    remainder = values
    for _ in range(pieces):
        upper = remainder.astype(BF)
        parts.append(upper)
        remainder = remainder - upper.astype(F32)
    return parts


def bias_matrix(pair_weight):
    parts = jnp.stack(split_parts(pair_weight, BIAS_PARTS))
    eye = jnp.eye(HALF, dtype=BF)
    full = parts.transpose(0, 2, 1)[:, :, None, None, :] * eye[None, None, :, :, None]
    return full.reshape(BIAS_PARTS * HEADS * HALF, HALF * pair_weight.shape[0])


def body(
    atom_single,
    token_single,
    tok_weight,
    atom_gain,
    w_query,
    w_key,
    w_value,
    pair_weight,
    out_weight,
    pair_feats,
    counts,
    atom_token,
    window_shift,
    atom_cot,
):
    seq = lax.axis_size("seq")
    rep = lax.axis_size("rep")
    seq_place = lax.axis_index("seq")
    rep_place = lax.axis_index("rep")
    group_place = seq_place * rep + rep_place
    atoms, width = atom_single.shape
    tok_rows = token_single.shape[0]
    half_rows = tok_rows // 2
    total_atoms = atoms * seq * rep
    smem = pl.BlockSpec(memory_space=pltpu.SMEM)

    proj = dot(token_single, tok_weight).astype(BF)
    below = lax.ppermute(proj[tok_rows - half_rows :], "seq", [(i, i + 1) for i in range(seq - 1)])
    tok_place = (seq_place * tok_rows - half_rows).reshape(1)
    tok2 = atom_token.reshape(atoms // SUB, SUB)
    gain = atom_gain.reshape(1, width)
    rows = min(1024, atoms)
    rim = jax.ShapeDtypeStruct((REACH, 2 * width), BF)
    hidden, query, key_values, first, last = pl.pallas_call(
        front_kernel,
        grid=(atoms // rows,),
        in_specs=[
            smem,
            smem,
            row_block(rows, width),
            whole(tok2.shape),
            whole(below.shape),
            whole(proj.shape),
            whole(gain.shape),
            whole(w_query.shape),
            whole(w_key.shape),
            whole(w_value.shape),
        ],
        out_specs=[
            row_block(rows, width),
            row_block(rows, width),
            row_block(rows, 2 * width),
            whole(rim.shape),
            whole(rim.shape),
        ],
        out_shape=[
            jax.ShapeDtypeStruct((atoms, width), F32),
            jax.ShapeDtypeStruct((atoms, width), BF),
            jax.ShapeDtypeStruct((atoms, 2 * width), BF),
            rim,
            rim,
        ],
        scratch_shapes=[pltpu.VMEM((half_rows + tok_rows + SPAN, width), BF)],
        compiler_params=pltpu.CompilerParams(vmem_limit_bytes=VMEM),
        name="front",
    )(tok2, tok_place, atom_single, tok2, below, proj, gain, w_query, w_key, w_value)

    count = seq * rep
    up = [(i, i + 1) for i in range(count - 1)]
    down = [(i + 1, i) for i in range(count - 1)]
    axes = ("seq", "rep")
    kv_low = lax.ppermute(last, axes, up)
    kv_high = lax.ppermute(first, axes, down)

    windows = atoms // QUERY_BLOCK
    step_rows = STEP_WINDOWS * QUERY_BLOCK
    channels = pair_feats.shape[1]
    pair2 = pair_feats.reshape(atoms * channels, KEY_SPAN)
    bias_weight = bias_matrix(pair_weight)
    win_place = jnp.stack([group_place * atoms - REACH, jnp.int32(total_atoms)])
    scratch = pltpu.VMEM((atoms + 2 * REACH, width), F32)
    atom_out, d_query, d_kv, d_low, d_high = pl.pallas_call(
        window_kernel,
        grid=(windows // STEP_WINDOWS,),
        in_specs=[
            smem,
            smem,
            whole(key_values.shape),
            whole(kv_low.shape),
            whole(kv_high.shape),
            row_block(step_rows, width),
            row_block(step_rows, width),
            row_block(step_rows, width),
            row_block(step_rows * channels, KEY_SPAN),
            whole(bias_weight.shape),
            whole(out_weight.shape),
        ],
        out_specs=[
            row_block(step_rows, width),
            row_block(step_rows, width),
            whole(key_values.shape),
            whole(kv_low.shape),
            whole(kv_high.shape),
        ],
        out_shape=[
            jax.ShapeDtypeStruct((atoms, width), BF),
            jax.ShapeDtypeStruct((atoms, width), BF),
            jax.ShapeDtypeStruct((atoms, 2 * width), BF),
            jax.ShapeDtypeStruct((REACH, 2 * width), BF),
            jax.ShapeDtypeStruct((REACH, 2 * width), BF),
        ],
        scratch_shapes=[scratch] * 4,
        compiler_params=pltpu.CompilerParams(vmem_limit_bytes=VMEM),
        name="windows",
    )(
        window_shift,
        win_place,
        key_values,
        kv_low,
        kv_high,
        query,
        hidden,
        atom_cot,
        pair2,
        bias_weight,
        out_weight,
    )

    rim_high = lax.ppermute(d_low, axes, down)
    rim_low = lax.ppermute(d_high, axes, up)
    tok_ext = half_rows + tok_rows
    sums = jax.ShapeDtypeStruct((tok_ext // 2, 2 * width), BF)
    core = rep_place % 2
    atom_grad, mine, other = pl.pallas_call(
        back_kernel,
        grid=(atoms // rows,),
        in_specs=[
            smem,
            smem,
            whole(tok2.shape),
            row_block(rows, width),
            row_block(rows, width),
            row_block(rows, width),
            row_block(rows, width),
            row_block(rows, 2 * width),
            whole(rim_low.shape),
            whole(rim_high.shape),
            whole(gain.shape),
            whole(w_query.shape),
            whole(w_key.shape),
            whole(w_value.shape),
        ],
        out_specs=[row_block(rows, width), whole(sums.shape), whole(sums.shape)],
        out_shape=[jax.ShapeDtypeStruct((atoms, width), BF), sums, sums],
        scratch_shapes=[pltpu.VMEM((tok_ext + SPAN, 2 * width), F32)],
        compiler_params=pltpu.CompilerParams(vmem_limit_bytes=VMEM),
        name="back",
    )(
        tok2,
        jnp.stack([tok_place[0], core]),
        tok2,
        atom_cot,
        hidden,
        atom_out,
        d_query,
        d_kv,
        rim_low,
        rim_high,
        gain,
        w_query,
        w_key,
        w_value,
    )

    quarter = tok_ext // 6
    swap = [(i, i ^ 1) for i in range(rep)]
    across = [(i, i ^ 2) for i in range(rep)]
    pair_sum = (mine.astype(F32) + lax.ppermute(other, "rep", swap).astype(F32)).astype(BF)
    low_part, own_part = pair_sum[:quarter], pair_sum[quarter:]
    straight = [(i, i - 1) for i in range(1, seq)]
    crossed = [((s + 1) * rep + r, s * rep + (r ^ 2)) for s in range(seq - 1) for r in range(rep)]
    got_own = lax.ppermute(own_part, "rep", across)
    got_straight = lax.ppermute(low_part, "seq", straight)
    got_crossed = lax.ppermute(low_part, axes, crossed)
    half_sum = own_part.astype(F32) + got_own.astype(F32)
    upper = half_sum[quarter:] + (got_straight.astype(F32) + got_crossed.astype(F32))
    half_sum = jnp.concatenate([half_sum[:quarter], upper], axis=0).astype(BF)
    other_sum = lax.ppermute(half_sum, "rep", swap)
    first = jnp.where(core == 0, half_sum, other_sum)
    second = jnp.where(core == 0, other_sum, half_sum)
    totals = jnp.concatenate(
        [first[:quarter], second[:quarter], first[quarter:], second[quarter:]], axis=0
    )
    token_grad = dot_nt(totals[:, :width], tok_weight).astype(BF)
    token_mean = (totals[:, width:].astype(F32) / counts.astype(F32)[:, None]).astype(BF)
    return (atom_out, token_mean, atom_grad, token_grad)


def solution(mesh):
    return jax.shard_map(
        body,
        mesh=mesh,
        in_specs=(
            P(("seq", "rep"), None),
            P("seq", None),
            P(),
            P(),
            P(),
            P(),
            P(),
            P(),
            P(),
            P(("seq", "rep"), None, None),
            P("seq"),
            P(("seq", "rep")),
            P(("seq", "rep")),
            P(("seq", "rep"), None),
        ),
        out_specs=(
            P(("seq", "rep"), None),
            P("seq", None),
            P(("seq", "rep"), None),
            P("seq", None),
        ),
        check_vma=False,
    )
```

```python
import jax
import jax.numpy as jnp
from jax import lax
from jax.experimental import pallas as pl
from jax.experimental.pallas import tpu as pltpu
from jax.sharding import PartitionSpec as P

HEADS = 4
QUERY_BLOCK = 32
KEY_SPAN = 128
REACH = KEY_SPAN - QUERY_BLOCK
RIM = 2 * REACH
RIM_WINDOWS = REACH // QUERY_BLOCK
HALF = QUERY_BLOCK // 2
SUB = 128
SPAN = 256
AUX = 16
STEP_WINDOWS = 16
BIAS_PARTS = 2
BF = jnp.bfloat16
F32 = jnp.float32
VMEM = 62 << 20


def dot(left, right):
    return jnp.dot(left, right, preferred_element_type=F32)


def dot_nt(left, right):
    return lax.dot_general(left, right, (((1,), (1,)), ((), ())), preferred_element_type=F32)


def dot_tn(left, right):
    return lax.dot_general(left, right, (((0,), (0,)), ((), ())), preferred_element_type=F32)


def whole(shape):
    return pl.BlockSpec(shape, lambda *_: (0,) * len(shape))


def row_block(rows, width):
    return pl.BlockSpec((rows, width), lambda i: (i, 0))


def fixed_block(rows, width, index):
    return pl.BlockSpec((rows, width), lambda *_: (index, 0))


def lagged_block(rows, width, count):
    return pl.BlockSpec((rows, width), lambda i: (jnp.clip(i - 1, 0, count - 1), 0))


def aligned(index, limit):
    return pl.multiple_of(jnp.clip(index, 0, limit - 1) // 16 * 16, 16)


def fill_table(table, below, proj, above):
    low, own = below.shape[0], proj.shape[0]
    table[0:low, :] = below[...]
    table[low : low + own, :] = proj[...]
    rest = table.shape[0] - low - own
    high = 0 if above is None else above.shape[0]
    if high:
        table[low + own : low + own + high, :] = above
    table[low + own + high :, :] = jnp.zeros((rest - high, table.shape[1]), BF)


def token_rows(ids, bases, table):
    lane = lax.broadcasted_iota(jnp.int32, (SUB, SPAN), 1).astype(F32)
    ids = [jnp.broadcast_to(row, (SUB, SUB)).T for row in ids]
    hot = [
        jnp.where(jnp.concatenate([row, row], axis=1) == lane, 1.0, 0.0).astype(BF) for row in ids
    ]
    return [dot(one, table[pl.ds(base, SPAN), :]) for one, base in zip(hot, bases)]


def centered(rows):
    center = rows - jnp.mean(rows, axis=-1, keepdims=True)
    spread = jnp.mean(center * center, axis=-1, keepdims=True)
    return center, lax.rsqrt(spread + 1e-05)


def pair_bias(pair, at, feats, bias_weight):
    both = jnp.concatenate([pair[at : at + feats, :], pair[at + feats : at + 2 * feats, :]], axis=1)
    parts = dot(bias_weight, both)
    heads = HEADS * HALF
    parts = parts[:heads] + parts[heads:]
    return jnp.concatenate([parts[:, :KEY_SPAN], parts[:, KEY_SPAN:]], axis=0)


def prep_kernel(
    shift_smem,
    proj,
    tok,
    pair_first,
    pair_last,
    cot_first,
    cot_last,
    atom_first,
    atom_last,
    bias_weight,
    down_out,
    up_out,
):
    feats = bias_weight.shape[1]
    blocks = tok.shape[0]
    windows = shift_smem.shape[0]
    rows = pair_first.shape[0] // (2 * feats)
    row = lax.broadcasted_iota(jnp.int32, (AUX, SUB), 0)
    lane = lax.broadcasted_iota(jnp.int32, (AUX, SUB), 1)
    for target, pair, lead, cot, cot_at, atom, block, window in (
        (down_out, pair_first, 0, cot_first, 0, atom_first, 0, 0),
        (
            up_out,
            pair_last,
            rows - RIM_WINDOWS,
            cot_last,
            cot_last.shape[0] - REACH,
            atom_last,
            blocks - 2,
            windows - RIM_WINDOWS,
        ),
    ):
        for k in range(RIM_WINDOWS):
            bias = pair_bias(pair, (lead + k) * 2 * feats, feats, bias_weight[...])
            upper = bias.astype(BF)
            target[2 * k * SUB : (2 * k + 1) * SUB, :] = upper
            target[(2 * k + 1) * SUB : (2 * k + 2) * SUB, :] = (bias - upper.astype(F32)).astype(BF)
        at = 2 * RIM_WINDOWS * SUB
        target[at : at + REACH, :] = cot[cot_at : cot_at + REACH, :]
        at += REACH
        target[at : at + 2 * SUB, :] = atom[...]
        at += 2 * SUB
        ids = [tok[block + k : block + k + 1, :] for k in range(2)]
        aux = jnp.zeros((AUX, SUB), F32)
        for k in range(2):
            aux = jnp.where(row == k, ((ids[k] >> 8) & 7).astype(F32), aux)
            aux = jnp.where(row == 2 + k, (ids[k] & 255).astype(F32), aux)
        for k in range(RIM_WINDOWS):
            aux = jnp.where(
                (row == 4) & (lane == k), shift_smem[window + k].astype(F32), aux
            )
        target[at : at + AUX, :] = aux.astype(BF)
    at = down_out.shape[0] - RIM
    down_out[at : at + RIM, :] = proj[...]


def front_kernel(
    tok_smem,
    place,
    atom,
    tok,
    below,
    proj,
    gain,
    w_query,
    w_key,
    w_value,
    hidden_out,
    query_out,
    kv_out,
    table,
):
    step = pl.program_id(0)
    limit = below.shape[0] + proj.shape[0]

    @pl.when(step == 0)
    def _():
        fill_table(table, below, proj, None)

    blocks = range(atom.shape[0] // SUB)
    bases = [aligned(tok_smem[step * len(blocks) + k, 0] - place[0], limit) for k in blocks]
    ids = [
        (tok[pl.ds(step * len(blocks) + k, 1), :] - (place[0] + bases[k])).astype(F32)
        for k in blocks
    ]
    hidden = atom[...].astype(F32) + jnp.concatenate(token_rows(ids, bases, table), axis=0)
    hidden_out[...] = hidden
    center, inv = centered(hidden)
    normed = (center * inv * gain[...]).astype(BF)
    query_out[...] = dot(normed, w_query[...]).astype(BF)
    keys = dot(normed, w_key[...]).astype(BF)
    values = dot(normed, w_value[...]).astype(BF)
    kv_out[...] = jnp.concatenate([keys, values], axis=1)


def head_lanes(width):
    return lax.broadcasted_iota(jnp.int32, (HALF, width), 1) // (width // HEADS)


def stacked(rows):
    lane = head_lanes(rows.shape[1])
    parts = []
    for half in range(2):
        piece = rows[half * HALF : (half + 1) * HALF, :]
        for h in range(HEADS):
            parts.append(jnp.where(lane == h, piece, jnp.zeros_like(piece)))
    return jnp.concatenate(parts, axis=0)


def unstacked(rows):
    lane = head_lanes(rows.shape[1])
    parts = []
    for half in range(2):
        piece = None
        for h in range(HEADS):
            at = (half * HEADS + h) * HALF
            part = rows[at : at + HALF, :]
            piece = part if piece is None else jnp.where(lane == h, part, piece)
        parts.append(piece)
    return jnp.concatenate(parts, axis=0)


def attend(starts, first, total, bias, query, d_attn, keys_s, values_s, dkeys_s, dvalues_s, wanted):
    width = query[0].shape[1]
    scale = (width // HEADS) ** (-0.5)
    each = range(len(starts))
    key_lane = lax.broadcasted_iota(jnp.int32, (1, KEY_SPAN), 1)
    ones = jnp.ones((KEY_SPAN, KEY_SPAN), BF)
    spots = [key_lane + (first + start) for start in starts]
    inside = [(spot >= 0) & (spot < total) for spot in spots]
    keys = [keys_s[pl.ds(start, KEY_SPAN), :].astype(BF) for start in starts]
    values = [values_s[pl.ds(start, KEY_SPAN), :].astype(BF) for start in starts]
    q_rows = [stacked(rows) for rows in query]
    g_rows = [stacked(rows) for rows in d_attn]
    bias = [make() for make in bias]
    scores = [
        jnp.where(inside[k], dot_nt(q_rows[k], keys[k]) * scale + bias[k], -1e30) for k in each
    ]
    weights = [jnp.exp(score - jnp.max(score, axis=-1, keepdims=True)) for score in scores]
    mixed = [dot(weights[k].astype(BF), jnp.concatenate([values[k], ones], axis=1)) for k in each]
    inverse = [1.0 / rows[:, width:] for rows in mixed]
    probs = [weights[k] * inverse[k] for k in each]
    attn = [unstacked(mixed[k][:, :width] * inverse[k]) for k in each] if wanted else None
    d_probs = [dot_nt(g_rows[k], values[k]) for k in each]
    joint = [probs[k] * d_probs[k] for k in each]
    d_scores = [joint[k] - probs[k] * dot(joint[k].astype(BF), ones) for k in each]
    d_scores = [(rows * scale).astype(BF) for rows in d_scores]
    d_values = [dot_tn(probs[k].astype(BF), g_rows[k]) for k in each]
    d_keys = [dot_tn(d_scores[k], q_rows[k]) for k in each]
    d_query = [unstacked(dot(d_scores[k], keys[k])).astype(BF) for k in each] if wanted else None
    for k in each:
        dkeys_s[pl.ds(starts[k], KEY_SPAN), :] += d_keys[k]
        dvalues_s[pl.ds(starts[k], KEY_SPAN), :] += d_values[k]
    return attn, d_query


def main_kernel(
    shift_smem,
    tok_smem,
    place,
    tok,
    low_buf,
    high_buf,
    below,
    proj,
    kv,
    query,
    hidden,
    cot,
    pair,
    bias_weight,
    out_weight,
    gain,
    w_query,
    w_key,
    w_value,
    out_ref,
    grad_ref,
    mine_ref,
    other_ref,
    table,
    keys_s,
    values_s,
    dkeys_s,
    dvalues_s,
    hidden_s,
    cot_s,
    out_s,
    dq_s,
    total_s,
):
    step = pl.program_id(0)
    last = pl.num_programs(0) - 1
    atoms, width = hidden_s.shape
    rows_in = query.shape[0]
    count = rows_in // QUERY_BLOCK
    tok_low, tok_first, core = place[0], place[1], place[2]
    first, total = place[3], place[4]
    tok_ext = total_s.shape[0] - SPAN
    limit = below.shape[0] + proj.shape[0]
    cot_at = 2 * RIM_WINDOWS * SUB
    atom_at = cot_at + REACH
    aux_at = atom_at + 2 * SUB

    def rim_bias(buf, k):
        at = 2 * k * SUB
        return buf[at : at + SUB, :].astype(F32) + buf[at + SUB : at + 2 * SUB, :].astype(F32)

    @pl.when(step == 0)
    def _():
        dkeys_s[...] = jnp.zeros_like(dkeys_s)
        dvalues_s[...] = jnp.zeros_like(dvalues_s)
        total_s[...] = jnp.zeros_like(total_s)
        fill_table(table, below, proj, high_buf[aux_at + AUX :, :])
        blocks = tok_smem.shape[0]
        ends = [
            tok_smem[0, 0] - tok_low - RIM,
            tok_smem[blocks - 1, SUB - 1] - tok_low,
        ]
        bufs = [low_buf, high_buf]
        ids, bases, atoms_in, shifts = [], [], [], []
        lane = lax.broadcasted_iota(jnp.int32, (1, SUB), 1)
        for buf, end in zip(bufs, ends):
            base = aligned(end, limit)
            offset = ((base + tok_low) & 2047).astype(F32)
            aux = buf[aux_at : aux_at + AUX, :].astype(F32)
            for k in range(2):
                part = aux[k : k + 1, :] * 256.0 + aux[2 + k : 3 + k, :] - offset
                ids.append(jnp.where(part < 0.0, part + 2048.0, part))
                bases.append(base)
            atoms_in.append(buf[atom_at : atom_at + 2 * SUB, :].astype(F32))
            for k in range(RIM_WINDOWS):
                value = jnp.sum(jnp.where(lane == k, aux[4:5, :], 0.0))
                shifts.append(value.astype(jnp.int32))
        rim = jnp.concatenate(atoms_in, axis=0) + jnp.concatenate(
            token_rows(ids, bases, table), axis=0
        )
        center, inv = centered(rim)
        normed = (center * inv * gain[...]).astype(BF)
        skip = 2 * SUB - RIM
        for target, weight, own in (
            (keys_s, w_key, slice(0, width)),
            (values_s, w_value, slice(width, 2 * width)),
        ):
            rows = dot(normed, weight[...]).astype(BF).astype(F32)
            target[0:RIM, :] = rows[skip : 2 * SUB]
            target[RIM : RIM + atoms, :] = kv[:, own].astype(F32)
            target[RIM + atoms :, :] = rows[2 * SUB : 2 * SUB + RIM]
        q_rim = dot(normed, w_query[...]).astype(BF)
        q_rim = [q_rim[2 * SUB - REACH : 2 * SUB], q_rim[2 * SUB : 2 * SUB + REACH]]
        starts, q_in, g_in, bias = [], [], [], []
        for side, buf in enumerate(bufs):
            grads = dot_nt(buf[cot_at : cot_at + REACH, :], out_weight[...]).astype(BF)
            for k in range(RIM_WINDOWS):
                at = slice(k * QUERY_BLOCK, (k + 1) * QUERY_BLOCK)
                origin = k * QUERY_BLOCK + (REACH + atoms if side else 0)
                shift = jnp.clip(shifts[side * RIM_WINDOWS + k], 0, REACH)
                starts.append(origin + shift)
                q_in.append(q_rim[side][at])
                g_in.append(grads[at])
                bias.append(lambda buf=buf, k=k: rim_bias(buf, k))
        attend(
            starts, first, total, bias, q_in, g_in, keys_s, values_s, dkeys_s, dvalues_s, False
        )

    @pl.when((step > 0) & (step < last))
    def _():
        group = step - 1
        at = pl.multiple_of(group * rows_in, rows_in)
        rows = pl.ds(at, rows_in)
        hidden_s[rows, :] = hidden[...]
        cot_s[rows, :] = cot[...]
        d_attn = dot_nt(cot[...], out_weight[...]).astype(BF)
        starts, q_in, g_in, bias = [], [], [], []
        feats = bias_weight.shape[1]
        for k in range(count):
            block = slice(k * QUERY_BLOCK, (k + 1) * QUERY_BLOCK)
            window = group * count + k
            starts.append(window * QUERY_BLOCK + REACH + shift_smem[window])
            q_in.append(query[block, :])
            g_in.append(d_attn[block, :])
            bias.append(lambda k=k: pair_bias(pair, 2 * k * feats, feats, bias_weight[...]))
        attn, d_query = attend(
            starts, first, total, bias, q_in, g_in, keys_s, values_s, dkeys_s, dvalues_s, True
        )
        dq_s[rows, :] = jnp.concatenate(d_query, axis=0)
        mixed = jnp.concatenate(attn, axis=0).astype(BF)
        out = (hidden[...] + dot(mixed, out_weight[...])).astype(BF)
        out_ref[...] = out
        out_s[rows, :] = out

    @pl.when(step == last)
    def _():
        reach = SUB + 16
        row = lax.broadcasted_iota(jnp.int32, (reach, SUB), 0)
        chunk = min(1024, atoms)
        blocks = range(chunk // SUB)
        for part in range(atoms // chunk):
            rows = slice(part * chunk, (part + 1) * chunk)
            ext = slice(RIM + part * chunk, RIM + (part + 1) * chunk)
            d_normed = dot_nt(dq_s[rows, :], w_query[...])
            d_normed += dot_nt(dkeys_s[ext, :].astype(BF), w_key[...])
            d_normed += dot_nt(dvalues_s[ext, :].astype(BF), w_value[...])
            center, inv = centered(hidden_s[rows, :])
            unit = center * inv
            scaled = d_normed * gain[...]
            d_front = inv * (
                scaled
                - jnp.mean(scaled, axis=-1, keepdims=True)
                - unit * jnp.mean(scaled * unit, axis=-1, keepdims=True)
            )
            grad = (cot_s[rows, :].astype(F32) + d_front).astype(BF)
            grad_ref[rows, :] = grad
            both = jnp.concatenate([grad, out_s[rows, :]], axis=1)
            lead = part * len(blocks)
            bases = [aligned(tok_smem[lead + k, 0] - tok_first, tok_ext) for k in blocks]
            ids = [tok[lead + k : lead + k + 1, :] - (tok_first + bases[k]) for k in blocks]
            hot = [jnp.where(row == line, 1.0, 0.0).astype(BF) for line in ids]
            sums = [dot(hot[k], both[k * SUB : (k + 1) * SUB, :]) for k in blocks]
            for k in blocks:
                total_s[pl.ds(bases[k], reach), :] += sums[k]
        quarter = tok_ext // 6
        for target, owner in ((mine_ref, core), (other_ref, 1 - core)):
            for k in range(3):
                at = pl.multiple_of((2 * k + owner) * quarter, quarter)
                target[k * quarter : (k + 1) * quarter, :] = total_s[pl.ds(at, quarter), :].astype(
                    BF
                )


def split_parts(values, pieces):
    parts = []
    remainder = values
    for _ in range(pieces):
        upper = remainder.astype(BF)
        parts.append(upper)
        remainder = remainder - upper.astype(F32)
    return parts


def bias_matrix(pair_weight):
    parts = jnp.stack(split_parts(pair_weight, BIAS_PARTS))
    eye = jnp.eye(HALF, dtype=BF)
    full = parts.transpose(0, 2, 1)[:, :, None, None, :] * eye[None, None, :, :, None]
    return full.reshape(BIAS_PARTS * HEADS * HALF, HALF * pair_weight.shape[0])


def body(
    atom_single,
    token_single,
    tok_weight,
    atom_gain,
    w_query,
    w_key,
    w_value,
    pair_weight,
    out_weight,
    pair_feats,
    counts,
    atom_token,
    window_shift,
    atom_cot,
):
    seq = lax.axis_size("seq")
    rep = lax.axis_size("rep")
    seq_place = lax.axis_index("seq")
    rep_place = lax.axis_index("rep")
    group_place = seq_place * rep + rep_place
    atoms, width = atom_single.shape
    tok_rows, tok_width = token_single.shape
    half_rows = tok_rows // 2
    below_rows = half_rows + RIM
    table_rows = below_rows + tok_rows + SPAN
    total_atoms = atoms * seq * rep
    windows = atoms // QUERY_BLOCK
    channels = pair_feats.shape[1]
    feats = QUERY_BLOCK * channels
    smem = pl.BlockSpec(memory_space=pltpu.SMEM)
    params = pltpu.CompilerParams(vmem_limit_bytes=VMEM)

    tok2 = atom_token.reshape(atoms // SUB, SUB)
    gain = atom_gain.reshape(1, width)
    pair2 = pair_feats.reshape(atoms * channels, KEY_SPAN)
    bias_weight = bias_matrix(pair_weight)
    core = rep_place % 2
    tok_first = seq_place * tok_rows - half_rows
    tok_low = tok_first - RIM
    place = jnp.stack(
        [tok_low, tok_first, core, group_place * atoms - RIM, jnp.int32(total_atoms)]
    ).astype(jnp.int32)

    proj = dot(token_single, tok_weight).astype(BF)
    below = lax.ppermute(
        proj[tok_rows - below_rows :], "seq", [(i, i + 1) for i in range(seq - 1)]
    )
    up_rows = 2 * RIM_WINDOWS * SUB + REACH + 2 * SUB + AUX
    edge = (RIM_WINDOWS + 1) * feats
    down_buf, up_buf = pl.pallas_call(
        prep_kernel,
        grid=(1,),
        in_specs=[
            smem,
            fixed_block(RIM, width, 0),
            whole(tok2.shape),
            fixed_block(edge, KEY_SPAN, 0),
            fixed_block(edge, KEY_SPAN, windows // (RIM_WINDOWS + 1) - 1),
            fixed_block(SUB, width, 0),
            fixed_block(SUB, width, atoms // SUB - 1),
            fixed_block(2 * SUB, width, 0),
            fixed_block(2 * SUB, width, atoms // (2 * SUB) - 1),
            whole(bias_weight.shape),
        ],
        out_specs=[
            whole((up_rows + RIM, width)),
            whole((up_rows, width)),
        ],
        out_shape=[
            jax.ShapeDtypeStruct((up_rows + RIM, width), BF),
            jax.ShapeDtypeStruct((up_rows, width), BF),
        ],
        compiler_params=params,
        cost_estimate=pl.CostEstimate(
            flops=atoms * width * 256, bytes_accessed=atoms * width * 32, transcendentals=0
        ),
        name="prep",
    )(
        window_shift,
        proj,
        tok2,
        pair2,
        pair2,
        atom_cot,
        atom_cot,
        atom_single,
        atom_single,
        bias_weight,
    )

    axes = ("seq", "rep")
    everyone = seq * rep
    low_buf = lax.ppermute(up_buf, axes, [(i, i + 1) for i in range(everyone - 1)])
    high_buf = lax.ppermute(down_buf, axes, [(i + 1, i) for i in range(everyone - 1)])

    rows = min(1024, atoms)
    hidden, query, key_values = pl.pallas_call(
        front_kernel,
        grid=(atoms // rows,),
        in_specs=[
            smem,
            smem,
            row_block(rows, width),
            whole(tok2.shape),
            whole(below.shape),
            whole(proj.shape),
            whole(gain.shape),
            whole(w_query.shape),
            whole(w_key.shape),
            whole(w_value.shape),
        ],
        out_specs=[row_block(rows, width), row_block(rows, width), row_block(rows, 2 * width)],
        out_shape=[
            jax.ShapeDtypeStruct((atoms, width), F32),
            jax.ShapeDtypeStruct((atoms, width), BF),
            jax.ShapeDtypeStruct((atoms, 2 * width), BF),
        ],
        scratch_shapes=[pltpu.VMEM((table_rows, width), BF)],
        compiler_params=params,
        cost_estimate=pl.CostEstimate(
            flops=atoms * width * 2000000, bytes_accessed=atoms * width * 12800, transcendentals=0
        ),
        name="front",
    )(tok2, place, atom_single, tok2, below, proj, gain, w_query, w_key, w_value)

    step_rows = STEP_WINDOWS * QUERY_BLOCK
    groups = windows // STEP_WINDOWS
    tok_ext = half_rows + tok_rows
    sums = jax.ShapeDtypeStruct((tok_ext // 2, 2 * width), BF)
    ext_rows = atoms + 2 * RIM
    atom_out, atom_grad, mine, other = pl.pallas_call(
        main_kernel,
        grid=(groups + 2,),
        in_specs=[
            smem,
            smem,
            smem,
            whole(tok2.shape),
            whole(low_buf.shape),
            whole(high_buf.shape),
            whole(below.shape),
            whole(proj.shape),
            whole(key_values.shape),
            lagged_block(step_rows, width, groups),
            lagged_block(step_rows, width, groups),
            lagged_block(step_rows, width, groups),
            lagged_block(step_rows * channels, KEY_SPAN, groups),
            whole(bias_weight.shape),
            whole(out_weight.shape),
            whole(gain.shape),
            whole(w_query.shape),
            whole(w_key.shape),
            whole(w_value.shape),
        ],
        out_specs=[
            lagged_block(step_rows, width, groups),
            whole((atoms, width)),
            whole(sums.shape),
            whole(sums.shape),
        ],
        out_shape=[
            jax.ShapeDtypeStruct((atoms, width), BF),
            jax.ShapeDtypeStruct((atoms, width), BF),
            sums,
            sums,
        ],
        scratch_shapes=[
            pltpu.VMEM((table_rows, width), BF),
            pltpu.VMEM((ext_rows, width), F32),
            pltpu.VMEM((ext_rows, width), F32),
            pltpu.VMEM((ext_rows, width), F32),
            pltpu.VMEM((ext_rows, width), F32),
            pltpu.VMEM((atoms, width), F32),
            pltpu.VMEM((atoms, width), BF),
            pltpu.VMEM((atoms, width), BF),
            pltpu.VMEM((atoms, width), BF),
            pltpu.VMEM((tok_ext + SPAN, 2 * width), F32),
        ],
        compiler_params=params,
        name="main",
    )(
        window_shift,
        tok2,
        place,
        tok2,
        low_buf,
        high_buf,
        below,
        proj,
        key_values,
        query,
        hidden,
        atom_cot,
        pair2,
        bias_weight,
        out_weight,
        gain,
        w_query,
        w_key,
        w_value,
    )

    quarter = tok_ext // 6
    swap = [(i, i ^ 1) for i in range(rep)]
    across = [(i, i ^ 2) for i in range(rep)]
    pair_sum = (mine.astype(F32) + lax.ppermute(other, "rep", swap).astype(F32)).astype(BF)
    low_part, own_part = pair_sum[:quarter], pair_sum[quarter:]
    straight = [(i, i - 1) for i in range(1, seq)]
    crossed = [((s + 1) * rep + r, s * rep + (r ^ 2)) for s in range(seq - 1) for r in range(rep)]
    got_straight = lax.ppermute(low_part, "seq", straight)
    got_crossed = lax.ppermute(low_part, axes, crossed)
    got_own = lax.ppermute(own_part, "rep", across)
    half_sum = own_part.astype(F32) + got_own.astype(F32)
    upper = half_sum[quarter:] + (got_straight.astype(F32) + got_crossed.astype(F32))
    half_sum = jnp.concatenate([half_sum[:quarter], upper], axis=0).astype(BF)
    other_sum = lax.ppermute(half_sum, "rep", swap)
    first = jnp.where(core == 0, half_sum, other_sum)
    second = jnp.where(core == 0, other_sum, half_sum)
    totals = jnp.concatenate(
        [first[:quarter], second[:quarter], first[quarter:], second[quarter:]], axis=0
    )
    token_grad = dot_nt(totals[:, :width], tok_weight).astype(BF)
    token_mean = (totals[:, width:].astype(F32) / counts.astype(F32)[:, None]).astype(BF)
    return (atom_out, token_mean, atom_grad, token_grad)


def solution(mesh):
    return jax.shard_map(
        body,
        mesh=mesh,
        in_specs=(
            P(("seq", "rep"), None),
            P("seq", None),
            P(),
            P(),
            P(),
            P(),
            P(),
            P(),
            P(),
            P(("seq", "rep"), None, None),
            P("seq"),
            P(("seq", "rep")),
            P(("seq", "rep")),
            P(("seq", "rep"), None),
        ),
        out_specs=(
            P(("seq", "rep"), None),
            P("seq", None),
            P(("seq", "rep"), None),
            P("seq", None),
        ),
        check_vma=False,
    )
```

```python
import jax
import jax.numpy as jnp
from jax import lax
from jax.experimental import pallas as pl
from jax.experimental.pallas import tpu as pltpu
from jax.sharding import PartitionSpec as P

HEADS = 4
QUERY_BLOCK = 32
KEY_SPAN = 128
REACH = KEY_SPAN - QUERY_BLOCK
RIM = 2 * REACH
RIM_WINDOWS = REACH // QUERY_BLOCK
HALF = QUERY_BLOCK // 2
SUB = 128
SPAN = 256
AUX = 16
STEP_WINDOWS = 16
BIAS_PARTS = 2
BF = jnp.bfloat16
F32 = jnp.float32
VMEM = 62 << 20


def dot(left, right):
    return jnp.dot(left, right, preferred_element_type=F32)


def dot_nt(left, right):
    return lax.dot_general(left, right, (((1,), (1,)), ((), ())), preferred_element_type=F32)


def dot_tn(left, right):
    return lax.dot_general(left, right, (((0,), (0,)), ((), ())), preferred_element_type=F32)


def whole(shape):
    return pl.BlockSpec(shape, lambda *_: (0,) * len(shape))


def fixed_block(rows, width, index):
    return pl.BlockSpec((rows, width), lambda *_: (index, 0))


def aligned(index, limit):
    return pl.multiple_of(jnp.clip(index, 0, limit - 1) // 16 * 16, 16)


def fill_table(table, below, proj, above):
    low, own = below.shape[0], proj.shape[0]
    table[0:low, :] = below[...]
    table[low : low + own, :] = proj[...]
    rest = table.shape[0] - low - own
    high = 0 if above is None else above.shape[0]
    if high:
        table[low + own : low + own + high, :] = above
    table[low + own + high :, :] = jnp.zeros((rest - high, table.shape[1]), BF)


def token_rows(ids, bases, table):
    lane = lax.broadcasted_iota(jnp.int32, (SUB, SPAN), 1).astype(F32)
    ids = [jnp.broadcast_to(row, (SUB, SUB)).T for row in ids]
    hot = [
        jnp.where(jnp.concatenate([row, row], axis=1) == lane, 1.0, 0.0).astype(BF) for row in ids
    ]
    return [dot(one, table[pl.ds(base, SPAN), :]) for one, base in zip(hot, bases)]


def centered(rows):
    center = rows - jnp.mean(rows, axis=-1, keepdims=True)
    spread = jnp.mean(center * center, axis=-1, keepdims=True)
    return center, lax.rsqrt(spread + 1e-05)


def pair_bias(pair, at, feats, bias_weight):
    both = jnp.concatenate(
        [pair[pl.ds(at, feats), :], pair[pl.ds(at + feats, feats), :]], axis=1
    )
    parts = dot(bias_weight, both)
    heads = HEADS * HALF
    parts = parts[:heads] + parts[heads:]
    return jnp.concatenate([parts[:, :KEY_SPAN], parts[:, KEY_SPAN:]], axis=0)


def bias_matrix(pair_weight):
    channels = pair_weight.shape[1]
    heads = HEADS * HALF
    wide = HALF * channels
    pick = lax.broadcasted_iota(jnp.int32, (heads, HEADS), 0) // HALF
    pick = (pick == lax.broadcasted_iota(jnp.int32, (heads, HEADS), 1)).astype(F32).astype(BF)
    copies = lax.broadcasted_iota(jnp.int32, (channels, wide), 1) % channels
    copies = copies == lax.broadcasted_iota(jnp.int32, (channels, wide), 0)
    copies = copies.astype(F32).astype(BF)
    row = lax.broadcasted_iota(jnp.int32, (heads, wide), 0) % HALF
    same = row == lax.broadcasted_iota(jnp.int32, (heads, wide), 1) // channels
    parts = []
    remainder = pair_weight
    for _ in range(BIAS_PARTS):
        upper = remainder.astype(BF)
        remainder = remainder - upper.astype(F32)
        rows = dot(pick, upper).astype(BF)
        parts.append(jnp.where(same, dot(rows, copies), 0.0).astype(BF))
    return jnp.concatenate(parts, axis=0)


def prep_kernel(
    shift_smem,
    proj,
    tok,
    pair_first,
    pair_last,
    cot_first,
    cot_last,
    atom_first,
    atom_last,
    pair_weight,
    bias_out,
    down_out,
    up_out,
):
    bias_weight = bias_matrix(pair_weight[...])
    bias_out[...] = bias_weight
    feats = bias_weight.shape[1]
    blocks = tok.shape[0]
    windows = shift_smem.shape[0]
    rows = pair_first.shape[0] // (2 * feats)
    row = lax.broadcasted_iota(jnp.int32, (AUX, SUB), 0)
    lane = lax.broadcasted_iota(jnp.int32, (AUX, SUB), 1)
    for target, pair, lead, cot, cot_at, atom, block, window in (
        (down_out, pair_first, 0, cot_first, 0, atom_first, 0, 0),
        (
            up_out,
            pair_last,
            rows - RIM_WINDOWS,
            cot_last,
            cot_last.shape[0] - REACH,
            atom_last,
            blocks - 2,
            windows - RIM_WINDOWS,
        ),
    ):
        for k in range(RIM_WINDOWS):
            bias = pair_bias(pair, (lead + k) * 2 * feats, feats, bias_weight)
            upper = bias.astype(BF)
            target[2 * k * SUB : (2 * k + 1) * SUB, :] = upper
            target[(2 * k + 1) * SUB : (2 * k + 2) * SUB, :] = (bias - upper.astype(F32)).astype(BF)
        at = 2 * RIM_WINDOWS * SUB
        target[at : at + REACH, :] = cot[cot_at : cot_at + REACH, :]
        at += REACH
        target[at : at + 2 * SUB, :] = atom[...]
        at += 2 * SUB
        ids = [tok[block + k : block + k + 1, :] for k in range(2)]
        aux = jnp.zeros((AUX, SUB), F32)
        for k in range(2):
            aux = jnp.where(row == k, ((ids[k] >> 8) & 7).astype(F32), aux)
            aux = jnp.where(row == 2 + k, (ids[k] & 255).astype(F32), aux)
        for k in range(RIM_WINDOWS):
            aux = jnp.where(
                (row == 4) & (lane == k), shift_smem[window + k].astype(F32), aux
            )
        target[at : at + AUX, :] = aux.astype(BF)
    at = down_out.shape[0] - RIM
    down_out[at : at + RIM, :] = proj[...]


def project(hidden, gain, w_query, w_key, w_value):
    center, inv = centered(hidden)
    normed = (center * inv * gain[...]).astype(BF)
    keys = dot(normed, w_key[...]).astype(BF).astype(F32)
    values = dot(normed, w_value[...]).astype(BF).astype(F32)
    return dot(normed, w_query[...]).astype(BF), keys, values


def front_kernel(
    tok_smem,
    tok,
    below,
    proj,
    atom,
    gain,
    w_query,
    w_key,
    w_value,
    hidden_out,
    query_out,
    keys_out,
    values_out,
    table,
):
    atoms = atom.shape[0]
    limit = below.shape[0] + proj.shape[0]
    tok_low = lax.axis_index("seq") * proj.shape[0] - below.shape[0]
    fill_table(table, below, proj, None)
    chunk = min(1024, atoms)
    blocks = range(chunk // SUB)
    for part in range(atoms // chunk):
        rows = slice(part * chunk, (part + 1) * chunk)
        lead = part * len(blocks)
        bases = [aligned(tok_smem[lead + k, 0] - tok_low, limit) for k in blocks]
        ids = [
            (tok[lead + k : lead + k + 1, :] - (tok_low + bases[k])).astype(F32) for k in blocks
        ]
        hidden = atom[rows, :].astype(F32) + jnp.concatenate(token_rows(ids, bases, table), axis=0)
        hidden_out[rows, :] = hidden
        query_out[rows, :], keys_out[rows, :], values_out[rows, :] = project(
            hidden, gain, w_query, w_key, w_value
        )


def head_lanes(width):
    return lax.broadcasted_iota(jnp.int32, (HALF, width), 1) // (width // HEADS)


def stacked(rows):
    lane = head_lanes(rows.shape[1])
    parts = []
    for half in range(2):
        piece = rows[half * HALF : (half + 1) * HALF, :]
        for h in range(HEADS):
            parts.append(jnp.where(lane == h, piece, jnp.zeros_like(piece)))
    return jnp.concatenate(parts, axis=0)


def unstacked(rows):
    lane = head_lanes(rows.shape[1])
    parts = []
    for half in range(2):
        piece = None
        for h in range(HEADS):
            at = (half * HEADS + h) * HALF
            part = rows[at : at + HALF, :]
            piece = part if piece is None else jnp.where(lane == h, part, piece)
        parts.append(piece)
    return jnp.concatenate(parts, axis=0)


def attend(starts, first, total, bias, query, d_attn, keys_s, values_s, dkeys_s, dvalues_s, wanted):
    width = query[0].shape[1]
    head = width // HEADS
    scale = head ** (-0.5)
    each = range(len(starts))
    key_lane = lax.broadcasted_iota(jnp.int32, (1, KEY_SPAN), 1)
    ones = jnp.ones((KEY_SPAN, KEY_SPAN), BF)
    spots = [key_lane + (first + start) for start in starts]
    inside = [(spot >= 0) & (spot < total) for spot in spots]
    keys = [keys_s[pl.ds(start, KEY_SPAN), :].astype(BF) for start in starts]
    values = [values_s[pl.ds(start, KEY_SPAN), :].astype(BF) for start in starts]
    q_rows = [stacked(rows) for rows in query]
    bias = [make() for make in bias]
    scores = [
        jnp.where(inside[k], dot_nt(q_rows[k], keys[k]) * scale + bias[k], -1e30) for k in each
    ]
    weights = [
        jnp.exp(score - jnp.max(score, axis=-1, keepdims=True)).astype(BF) for score in scores
    ]
    mixed = [dot(weights[k], jnp.concatenate([values[k], ones], axis=1)) for k in each]
    inverse = [1.0 / unstacked(rows[:, width:]) for rows in mixed]
    attn = [unstacked(mixed[k][:, :width]) * inverse[k] for k in each]
    attn = jnp.concatenate(attn, axis=0)
    inverse = jnp.concatenate(inverse, axis=0)
    row_head = lax.broadcasted_iota(jnp.int32, (width, width), 0) // head
    lane_head = lax.broadcasted_iota(jnp.int32, (width, width), 1) // head
    spread = jnp.where(row_head == lane_head, 1.0 / head, 0.0).astype(BF)
    shared = (dot((d_attn * attn).astype(BF), spread) * inverse).astype(BF)
    scaled = (d_attn * inverse).astype(BF)
    g_rows, s_rows = [], []
    for k in each:
        block = slice(k * QUERY_BLOCK, (k + 1) * QUERY_BLOCK)
        g_rows.append(stacked(scaled[block, :]))
        s_rows.append(stacked(shared[block, :]))
    d_probs = [
        dot_nt(
            jnp.concatenate([g_rows[k], s_rows[k]], axis=1),
            jnp.concatenate([values[k], -ones], axis=1),
        )
        for k in each
    ]
    d_scores = [(weights[k].astype(F32) * d_probs[k]).astype(BF) for k in each]
    d_values = [dot_tn(weights[k], g_rows[k]) for k in each]
    d_keys = [dot_tn(d_scores[k], q_rows[k]) for k in each]
    d_query = None
    if wanted:
        d_query = [unstacked(dot(d_scores[k], keys[k])) * scale for k in each]
        d_query = jnp.concatenate(d_query, axis=0).astype(BF)
    for k in each:
        dkeys_s[pl.ds(starts[k], KEY_SPAN), :] += d_keys[k]
        dvalues_s[pl.ds(starts[k], KEY_SPAN), :] += d_values[k]
    return attn, d_query


def main_kernel(
    shift_smem,
    tok_smem,
    tok,
    low_buf,
    high_buf,
    below,
    proj,
    query,
    hidden,
    cot,
    keys,
    values,
    pair,
    bias_weight,
    out_weight,
    gain,
    w_query,
    w_key,
    w_value,
    out_ref,
    grad_ref,
    mine_ref,
    other_ref,
    table,
    pair_s,
    keys_s,
    values_s,
    dkeys_s,
    dvalues_s,
    dq_s,
    total_s,
    sems,
):
    atoms, width = hidden.shape
    head = width // HEADS
    groups = sems.shape[0] - 2
    pair_rows = pair.shape[0] // groups
    rows_in = atoms // groups
    count = rows_in // QUERY_BLOCK
    feats = bias_weight.shape[1]
    tok_ext = total_s.shape[0] - SPAN
    limit = below.shape[0] + proj.shape[0]
    seq_place, rep_place = lax.axis_index("seq"), lax.axis_index("rep")
    rep = lax.axis_size("rep")
    group_place = seq_place * rep + rep_place
    tok_first = seq_place * proj.shape[0] - (below.shape[0] - RIM)
    tok_low = tok_first - RIM
    core = rep_place % 2
    first = group_place * atoms - RIM
    total = atoms * lax.axis_size("seq") * rep
    cot_at = 2 * RIM_WINDOWS * SUB
    atom_at = cot_at + REACH
    aux_at = atom_at + 2 * SUB

    def pair_copy(group):
        rows = pl.ds(pl.multiple_of(group * pair_rows, pair_rows), pair_rows)
        return pltpu.make_async_copy(pair.at[rows, :], pair_s.at[rows, :], sems.at[group])

    own = pl.ds(RIM, atoms)
    key_copy = pltpu.make_async_copy(keys, keys_s.at[own, :], sems.at[groups])
    value_copy = pltpu.make_async_copy(values, values_s.at[own, :], sems.at[groups + 1])
    key_copy.start()
    value_copy.start()
    for group in range(groups):
        pair_copy(group).start()

    dkeys_s[...] = jnp.zeros_like(dkeys_s)
    dvalues_s[...] = jnp.zeros_like(dvalues_s)
    total_s[...] = jnp.zeros_like(total_s)
    fill_table(table, below, proj, high_buf[aux_at + AUX :, :])

    ends = [
        tok_smem[0, 0] - tok_low - RIM,
        tok_smem[tok_smem.shape[0] - 1, SUB - 1] - tok_low,
    ]
    bufs = [low_buf, high_buf]
    ids, bases, atoms_in, shifts = [], [], [], []
    lane = lax.broadcasted_iota(jnp.int32, (1, SUB), 1)
    for buf, end in zip(bufs, ends):
        base = aligned(end, limit)
        offset = ((base + tok_low) & 2047).astype(F32)
        aux = buf[aux_at : aux_at + AUX, :].astype(F32)
        for k in range(2):
            part = aux[k : k + 1, :] * 256.0 + aux[2 + k : 3 + k, :] - offset
            ids.append(jnp.where(part < 0.0, part + 2048.0, part))
            bases.append(base)
        atoms_in.append(buf[atom_at : atom_at + 2 * SUB, :].astype(F32))
        for k in range(RIM_WINDOWS):
            value = jnp.sum(jnp.where(lane == k, aux[4:5, :], 0.0))
            shifts.append(jnp.clip(value.astype(jnp.int32), 0, REACH))
    rim = jnp.concatenate(atoms_in, axis=0)
    rim += jnp.concatenate(token_rows(ids, bases, table), axis=0)
    q_rim, k_rim, v_rim = project(rim, gain, w_query, w_key, w_value)
    skip = 2 * SUB - RIM
    for target, rows in ((keys_s, k_rim), (values_s, v_rim)):
        target[0:RIM, :] = rows[skip : 2 * SUB]
        target[RIM + atoms :, :] = rows[2 * SUB : 2 * SUB + RIM]

    def rim_bias(buf, k):
        at = 2 * k * SUB
        return buf[at : at + SUB, :].astype(F32) + buf[at + SUB : at + 2 * SUB, :].astype(F32)

    starts, q_in, bias = [], [], []
    for side, buf in enumerate(bufs):
        q_at = 2 * SUB if side else 2 * SUB - REACH
        for k in range(RIM_WINDOWS):
            origin = k * QUERY_BLOCK + (REACH + atoms if side else 0)
            starts.append(origin + shifts[side * RIM_WINDOWS + k])
            at = q_at + k * QUERY_BLOCK
            q_in.append(q_rim[at : at + QUERY_BLOCK])
            bias.append(lambda buf=buf, k=k: rim_bias(buf, k))
    cots = [buf[cot_at : cot_at + REACH, :] for buf in bufs]
    grads = dot_nt(jnp.concatenate(cots, axis=0), out_weight[...])
    key_copy.wait()
    value_copy.wait()
    attend(starts, first, total, bias, q_in, grads, keys_s, values_s, dkeys_s, dvalues_s, False)

    def work(group, carry):
        pair_copy(group).wait()
        rows = pl.ds(pl.multiple_of(group * rows_in, rows_in), rows_in)
        queries = query[rows, :]
        starts, q_in, bias = [], [], []
        for k in range(count):
            window = group * count + k
            starts.append(window * QUERY_BLOCK + REACH + shift_smem[window])
            q_in.append(queries[k * QUERY_BLOCK : (k + 1) * QUERY_BLOCK, :])
            at = pl.multiple_of(group * pair_rows + 2 * k * feats, feats)
            bias.append(lambda at=at: pair_bias(pair_s, at, feats, bias_weight[...]))
        grads = dot_nt(cot[rows, :], out_weight[...])
        attn, d_query = attend(
            starts, first, total, bias, q_in, grads, keys_s, values_s, dkeys_s, dvalues_s, True
        )
        dq_s[rows, :] = d_query
        out_ref[rows, :] = (hidden[rows, :] + dot(attn.astype(BF), out_weight[...])).astype(BF)
        return carry

    lax.fori_loop(0, groups, work, 0)

    scale = head ** (-0.5)
    chunk = min(1024, atoms)
    blocks = range(chunk // SUB)
    reach = SUB + 16
    row = lax.broadcasted_iota(jnp.int32, (reach, SUB), 0)
    for part in range(atoms // chunk):
        rows = slice(part * chunk, (part + 1) * chunk)
        ext = slice(RIM + part * chunk, RIM + (part + 1) * chunk)
        d_normed = dot_nt(dq_s[rows, :], w_query[...])
        d_normed += dot_nt((dkeys_s[ext, :] * scale).astype(BF), w_key[...])
        d_normed += dot_nt(dvalues_s[ext, :].astype(BF), w_value[...])
        center, inv = centered(hidden[rows, :])
        unit = center * inv
        scaled = d_normed * gain[...]
        d_front = inv * (
            scaled
            - jnp.mean(scaled, axis=-1, keepdims=True)
            - unit * jnp.mean(scaled * unit, axis=-1, keepdims=True)
        )
        grad = (cot[rows, :].astype(F32) + d_front).astype(BF)
        grad_ref[rows, :] = grad
        both = jnp.concatenate([grad, out_ref[rows, :]], axis=1)
        lead = part * len(blocks)
        bases = [aligned(tok_smem[lead + k, 0] - tok_first, tok_ext) for k in blocks]
        ids = [tok[lead + k : lead + k + 1, :] - (tok_first + bases[k]) for k in blocks]
        hot = [jnp.where(row == line, 1.0, 0.0).astype(BF) for line in ids]
        sums = [dot(hot[k], both[k * SUB : (k + 1) * SUB, :]) for k in blocks]
        for k in blocks:
            total_s[pl.ds(bases[k], reach), :] += sums[k]
    quarter = tok_ext // 6
    for target, owner in ((mine_ref, core), (other_ref, 1 - core)):
        for k in range(3):
            at = pl.multiple_of((2 * k + owner) * quarter, quarter)
            target[k * quarter : (k + 1) * quarter, :] = total_s[pl.ds(at, quarter), :].astype(BF)


def body(
    atom_single,
    token_single,
    tok_weight,
    atom_gain,
    w_query,
    w_key,
    w_value,
    pair_weight,
    out_weight,
    pair_feats,
    counts,
    atom_token,
    window_shift,
    atom_cot,
):
    seq = lax.axis_size("seq")
    rep = lax.axis_size("rep")
    rep_place = lax.axis_index("rep")
    atoms, width = atom_single.shape
    tok_rows, tok_width = token_single.shape
    half_rows = tok_rows // 2
    below_rows = half_rows + RIM
    table_rows = below_rows + tok_rows + SPAN
    windows = atoms // QUERY_BLOCK
    channels = pair_feats.shape[1]
    feats = QUERY_BLOCK * channels
    smem = pl.BlockSpec(memory_space=pltpu.SMEM)
    params = pltpu.CompilerParams(vmem_limit_bytes=VMEM)

    tok2 = atom_token.reshape(atoms // SUB, SUB)
    gain = atom_gain.reshape(1, width)
    pair2 = pair_feats.reshape(atoms * channels, KEY_SPAN)
    bias_shape = (BIAS_PARTS * HEADS * HALF, HALF * channels)
    core = rep_place % 2
    proj = dot(token_single, tok_weight).astype(BF)
    below = lax.ppermute(
        proj[tok_rows - below_rows :], "seq", [(i, i + 1) for i in range(seq - 1)]
    )
    up_rows = 2 * RIM_WINDOWS * SUB + REACH + 2 * SUB + AUX
    edge = (RIM_WINDOWS + 1) * feats
    bias_weight, down_buf, up_buf = pl.pallas_call(
        prep_kernel,
        grid=(1,),
        in_specs=[
            smem,
            fixed_block(RIM, width, 0),
            whole(tok2.shape),
            fixed_block(edge, KEY_SPAN, 0),
            fixed_block(edge, KEY_SPAN, windows // (RIM_WINDOWS + 1) - 1),
            fixed_block(SUB, width, 0),
            fixed_block(SUB, width, atoms // SUB - 1),
            fixed_block(2 * SUB, width, 0),
            fixed_block(2 * SUB, width, atoms // (2 * SUB) - 1),
            whole(pair_weight.shape[::-1]),
        ],
        out_specs=[
            whole(bias_shape),
            whole((up_rows + RIM, width)),
            whole((up_rows, width)),
        ],
        out_shape=[
            jax.ShapeDtypeStruct(bias_shape, BF),
            jax.ShapeDtypeStruct((up_rows + RIM, width), BF),
            jax.ShapeDtypeStruct((up_rows, width), BF),
        ],
        compiler_params=params,
        cost_estimate=pl.CostEstimate(
            flops=atoms * width * 256, bytes_accessed=atoms * width * 32, transcendentals=0
        ),
        name="prep",
    )(
        window_shift,
        proj,
        tok2,
        pair2,
        pair2,
        atom_cot,
        atom_cot,
        atom_single,
        atom_single,
        pair_weight.T,
    )

    axes = ("seq", "rep")
    everyone = seq * rep
    low_buf = lax.ppermute(up_buf, axes, [(i, i + 1) for i in range(everyone - 1)])
    high_buf = lax.ppermute(down_buf, axes, [(i + 1, i) for i in range(everyone - 1)])

    vmem = pl.BlockSpec(memory_space=pltpu.VMEM)
    hbm = pl.BlockSpec(memory_space=pl.ANY)
    rows_f32 = jax.ShapeDtypeStruct((atoms, width), F32)
    rows_bf = jax.ShapeDtypeStruct((atoms, width), BF)
    hidden, query, keys, values = pl.pallas_call(
        front_kernel,
        in_specs=[smem] + [vmem] * 8,
        out_specs=[vmem] * 4,
        out_shape=[rows_f32, rows_bf, rows_f32, rows_f32],
        scratch_shapes=[pltpu.VMEM((table_rows, width), BF)],
        compiler_params=params,
        cost_estimate=pl.CostEstimate(
            flops=atoms * width * 2000000, bytes_accessed=atoms * width * 12800, transcendentals=0
        ),
        name="front",
    )(tok2, tok2, below, proj, atom_single, gain, w_query, w_key, w_value)

    tok_ext = half_rows + tok_rows
    sums = jax.ShapeDtypeStruct((tok_ext // 2, 2 * width), BF)
    ext = pltpu.VMEM((atoms + 2 * RIM, width), F32)
    atom_out, atom_grad, mine, other = pl.pallas_call(
        main_kernel,
        in_specs=[smem, smem] + [vmem] * 8 + [hbm] * 3 + [vmem] * 6,
        out_specs=[vmem] * 4,
        out_shape=[rows_bf, rows_bf, sums, sums],
        scratch_shapes=[
            pltpu.VMEM((table_rows, width), BF),
            pltpu.VMEM(pair2.shape, BF),
            ext,
            ext,
            ext,
            ext,
            pltpu.VMEM((atoms, width), BF),
            pltpu.VMEM((tok_ext + SPAN, 2 * width), F32),
            pltpu.SemaphoreType.DMA((windows // STEP_WINDOWS + 2,)),
        ],
        compiler_params=params,
        name="main",
    )(
        window_shift,
        tok2,
        tok2,
        low_buf,
        high_buf,
        below,
        proj,
        query,
        hidden,
        atom_cot,
        keys,
        values,
        pair2,
        bias_weight,
        out_weight,
        gain,
        w_query,
        w_key,
        w_value,
    )

    quarter = tok_ext // 6
    swap = [(i, i ^ 1) for i in range(rep)]
    across = [(i, i ^ 2) for i in range(rep)]
    pair_sum = (mine.astype(F32) + lax.ppermute(other, "rep", swap).astype(F32)).astype(BF)
    low_part, own_part = pair_sum[:quarter], pair_sum[quarter:]
    straight = [(i, i - 1) for i in range(1, seq)]
    crossed = [((s + 1) * rep + r, s * rep + (r ^ 2)) for s in range(seq - 1) for r in range(rep)]
    got_straight = lax.ppermute(low_part, "seq", straight)
    got_crossed = lax.ppermute(low_part, axes, crossed)
    got_own = lax.ppermute(own_part, "rep", across)
    half_sum = own_part.astype(F32) + got_own.astype(F32)
    upper = half_sum[quarter:] + (got_straight.astype(F32) + got_crossed.astype(F32))
    half_sum = jnp.concatenate([half_sum[:quarter], upper], axis=0).astype(BF)
    other_sum = lax.ppermute(half_sum, "rep", swap)
    first = jnp.where(core == 0, half_sum, other_sum)
    second = jnp.where(core == 0, other_sum, half_sum)
    totals = jnp.concatenate(
        [first[:quarter], second[:quarter], first[quarter:], second[quarter:]], axis=0
    )
    token_grad = dot_nt(totals[:, :width], tok_weight).astype(BF)
    token_mean = (totals[:, width:].astype(F32) / counts.astype(F32)[:, None]).astype(BF)
    return (atom_out, token_mean, atom_grad, token_grad)


def solution(mesh):
    return jax.shard_map(
        body,
        mesh=mesh,
        in_specs=(
            P(("seq", "rep"), None),
            P("seq", None),
            P(),
            P(),
            P(),
            P(),
            P(),
            P(),
            P(),
            P(("seq", "rep"), None, None),
            P("seq"),
            P(("seq", "rep")),
            P(("seq", "rep")),
            P(("seq", "rep"), None),
        ),
        out_specs=(
            P(("seq", "rep"), None),
            P("seq", None),
            P(("seq", "rep"), None),
            P("seq", None),
        ),
        check_vma=False,
    )
```

```python
import jax
import jax.numpy as jnp
from jax import lax
from jax.experimental import pallas as pl
from jax.experimental.pallas import tpu as pltpu
from jax.sharding import PartitionSpec as P

HEADS = 4
QUERY_BLOCK = 32
KEY_SPAN = 128
REACH = KEY_SPAN - QUERY_BLOCK
RIM = 2 * REACH
RIM_WINDOWS = REACH // QUERY_BLOCK
HALF = QUERY_BLOCK // 2
SUB = 128
SPAN = 256
AUX = 16
STEP_WINDOWS = 16
BIAS_PARTS = 2
BF = jnp.bfloat16
F32 = jnp.float32
VMEM = 62 << 20


def dot(left, right):
    return jnp.dot(left, right, preferred_element_type=F32)


def dot_nt(left, right):
    return lax.dot_general(left, right, (((1,), (1,)), ((), ())), preferred_element_type=F32)


def dot_tn(left, right):
    return lax.dot_general(left, right, (((0,), (0,)), ((), ())), preferred_element_type=F32)


def whole(shape):
    return pl.BlockSpec(shape, lambda *_: (0,) * len(shape))


def fixed_block(rows, width, index):
    return pl.BlockSpec((rows, width), lambda *_: (index, 0))


def aligned(index, limit):
    return pl.multiple_of(jnp.clip(index, 0, limit - 1) // 16 * 16, 16)


def rows_copy(source, target, at, sem):
    return pltpu.make_async_copy(source, target.at[pl.ds(at, source.shape[0]), :], sem)


def fill_table(table, below, proj, above):
    low, own = below.shape[0], proj.shape[0]
    table[0:low, :] = below[...]
    table[low : low + own, :] = proj[...]
    rest = table.shape[0] - low - own
    high = 0 if above is None else above.shape[0]
    if high:
        table[low + own : low + own + high, :] = above
    table[low + own + high :, :] = jnp.zeros((rest - high, table.shape[1]), BF)


def token_rows(ids, bases, table):
    lane = lax.broadcasted_iota(jnp.int32, (SUB, SPAN), 1).astype(F32)
    ids = [jnp.broadcast_to(row, (SUB, SUB)).T for row in ids]
    hot = [
        jnp.where(jnp.concatenate([row, row], axis=1) == lane, 1.0, 0.0).astype(BF) for row in ids
    ]
    return [dot(one, table[pl.ds(base, SPAN), :]) for one, base in zip(hot, bases)]


def centered(rows):
    center = rows - jnp.mean(rows, axis=-1, keepdims=True)
    spread = jnp.mean(center * center, axis=-1, keepdims=True)
    return center, lax.rsqrt(spread + 1e-05)


def pair_bias(pair, at, feats, bias_weight):
    both = jnp.concatenate(
        [pair[pl.ds(at, feats), :], pair[pl.ds(at + feats, feats), :]], axis=1
    )
    parts = dot(bias_weight, both)
    heads = HEADS * HALF
    parts = parts[:heads] + parts[heads:]
    return jnp.concatenate([parts[:, :KEY_SPAN], parts[:, KEY_SPAN:]], axis=0)


def bias_matrix(pair_weight):
    channels = pair_weight.shape[1]
    heads = HEADS * HALF
    wide = HALF * channels
    pick = lax.broadcasted_iota(jnp.int32, (heads, HEADS), 0) // HALF
    pick = (pick == lax.broadcasted_iota(jnp.int32, (heads, HEADS), 1)).astype(F32).astype(BF)
    copies = lax.broadcasted_iota(jnp.int32, (channels, wide), 1) % channels
    copies = copies == lax.broadcasted_iota(jnp.int32, (channels, wide), 0)
    copies = copies.astype(F32).astype(BF)
    row = lax.broadcasted_iota(jnp.int32, (heads, wide), 0) % HALF
    same = row == lax.broadcasted_iota(jnp.int32, (heads, wide), 1) // channels
    parts = []
    remainder = pair_weight
    for _ in range(BIAS_PARTS):
        upper = remainder.astype(BF)
        remainder = remainder - upper.astype(F32)
        rows = dot(pick, upper).astype(BF)
        parts.append(jnp.where(same, dot(rows, copies), 0.0).astype(BF))
    return jnp.concatenate(parts, axis=0)


def prep_kernel(
    shift_smem,
    proj,
    tok,
    pair_first,
    pair_last,
    cot_first,
    cot_last,
    atom_first,
    atom_last,
    pair_weight,
    bias_out,
    down_out,
    up_out,
):
    bias_weight = bias_matrix(pair_weight[...])
    bias_out[...] = bias_weight
    feats = bias_weight.shape[1]
    blocks = tok.shape[0]
    windows = shift_smem.shape[0]
    rows = pair_first.shape[0] // (2 * feats)
    row = lax.broadcasted_iota(jnp.int32, (AUX, SUB), 0)
    lane = lax.broadcasted_iota(jnp.int32, (AUX, SUB), 1)
    for target, pair, lead, cot, cot_at, atom, block, window in (
        (down_out, pair_first, 0, cot_first, 0, atom_first, 0, 0),
        (
            up_out,
            pair_last,
            rows - RIM_WINDOWS,
            cot_last,
            cot_last.shape[0] - REACH,
            atom_last,
            blocks - 2,
            windows - RIM_WINDOWS,
        ),
    ):
        for k in range(RIM_WINDOWS):
            bias = pair_bias(pair, (lead + k) * 2 * feats, feats, bias_weight)
            upper = bias.astype(BF)
            target[2 * k * SUB : (2 * k + 1) * SUB, :] = upper
            target[(2 * k + 1) * SUB : (2 * k + 2) * SUB, :] = (bias - upper.astype(F32)).astype(BF)
        at = 2 * RIM_WINDOWS * SUB
        target[at : at + REACH, :] = cot[cot_at : cot_at + REACH, :]
        at += REACH
        target[at : at + 2 * SUB, :] = atom[...]
        at += 2 * SUB
        ids = [tok[block + k : block + k + 1, :] for k in range(2)]
        aux = jnp.zeros((AUX, SUB), F32)
        for k in range(2):
            aux = jnp.where(row == k, ((ids[k] >> 8) & 7).astype(F32), aux)
            aux = jnp.where(row == 2 + k, (ids[k] & 255).astype(F32), aux)
        for k in range(RIM_WINDOWS):
            aux = jnp.where(
                (row == 4) & (lane == k), shift_smem[window + k].astype(F32), aux
            )
        target[at : at + AUX, :] = aux.astype(BF)
    at = down_out.shape[0] - RIM
    down_out[at : at + RIM, :] = proj[...]


def project(hidden, gain, w_query, w_key, w_value):
    center, inv = centered(hidden)
    normed = (center * inv * gain[...]).astype(BF)
    keys = dot(normed, w_key[...]).astype(BF).astype(F32)
    values = dot(normed, w_value[...]).astype(BF).astype(F32)
    return dot(normed, w_query[...]).astype(BF), keys, values


def front_kernel(
    tok_smem,
    tok,
    below,
    proj,
    atom,
    gain,
    w_query,
    w_key,
    w_value,
    bias_weight,
    pair,
    hidden_out,
    query_out,
    keys_out,
    values_out,
    bias_out,
    table,
    weight_s,
    pair_s,
    sems,
):
    atoms = atom.shape[0]
    groups = sems.shape[0] - 3
    pair_rows = pair_s.shape[0] // groups
    copies = [
        rows_copy(below, table, 0, sems.at[groups]),
        rows_copy(proj, table, below.shape[0], sems.at[groups + 1]),
        pltpu.make_async_copy(bias_weight, weight_s, sems.at[groups + 2]),
    ]
    for copy in copies:
        copy.start()

    def pair_copy(group):
        rows = pl.ds(pl.multiple_of(group * pair_rows, pair_rows), pair_rows)
        return pltpu.make_async_copy(pair.at[rows, :], pair_s.at[rows, :], sems.at[group])

    for group in range(groups):
        pair_copy(group).start()
    limit = below.shape[0] + proj.shape[0]
    tok_low = lax.axis_index("seq") * proj.shape[0] - below.shape[0]
    table[limit:, :] = jnp.zeros((table.shape[0] - limit, table.shape[1]), BF)
    for copy in copies[:2]:
        copy.wait()
    chunk = min(1024, atoms)
    blocks = range(chunk // SUB)
    for part in range(atoms // chunk):
        rows = slice(part * chunk, (part + 1) * chunk)
        lead = part * len(blocks)
        bases = [aligned(tok_smem[lead + k, 0] - tok_low, limit) for k in blocks]
        ids = [
            (tok[lead + k : lead + k + 1, :] - (tok_low + bases[k])).astype(F32) for k in blocks
        ]
        hidden = atom[rows, :].astype(F32) + jnp.concatenate(token_rows(ids, bases, table), axis=0)
        hidden_out[rows, :] = hidden
        query_out[rows, :], keys_out[rows, :], values_out[rows, :] = project(
            hidden, gain, w_query, w_key, w_value
        )
    copies[2].wait()
    feats = weight_s.shape[1]
    count = pair_rows // (2 * feats)

    def work(group, carry):
        pair_copy(group).wait()
        for k in range(count):
            window = group * count + k
            at = pl.multiple_of(window * 2 * feats, feats)
            rows = pl.ds(pl.multiple_of(window * SUB, SUB), SUB)
            bias_out[rows, :] = pair_bias(pair_s, at, feats, weight_s[...])
        return carry

    lax.fori_loop(0, groups, work, 0)


def head_lanes(width):
    return lax.broadcasted_iota(jnp.int32, (HALF, width), 1) // (width // HEADS)


def stacked(rows):
    lane = head_lanes(rows.shape[1])
    parts = []
    for half in range(2):
        piece = rows[half * HALF : (half + 1) * HALF, :]
        for h in range(HEADS):
            parts.append(jnp.where(lane == h, piece, jnp.zeros_like(piece)))
    return jnp.concatenate(parts, axis=0)


def unstacked(rows):
    lane = head_lanes(rows.shape[1])
    parts = []
    for half in range(2):
        piece = None
        for h in range(HEADS):
            at = (half * HEADS + h) * HALF
            part = rows[at : at + HALF, :]
            piece = part if piece is None else jnp.where(lane == h, part, piece)
        parts.append(piece)
    return jnp.concatenate(parts, axis=0)


def attend(starts, first, total, bias, query, d_attn, keys_s, values_s, dkeys_s, dvalues_s, wanted):
    width = query[0].shape[1]
    head = width // HEADS
    scale = head ** (-0.5)
    each = range(len(starts))
    key_lane = lax.broadcasted_iota(jnp.int32, (1, KEY_SPAN), 1)
    ones = jnp.ones((KEY_SPAN, KEY_SPAN), BF)
    spots = [key_lane + (first + start) for start in starts]
    inside = [(spot >= 0) & (spot < total) for spot in spots]
    keys = [keys_s[pl.ds(start, KEY_SPAN), :].astype(BF) for start in starts]
    values = [values_s[pl.ds(start, KEY_SPAN), :].astype(BF) for start in starts]
    q_rows = [stacked(rows) for rows in query]
    bias = [make() for make in bias]
    scores = [
        jnp.where(inside[k], dot_nt(q_rows[k], keys[k]) * scale + bias[k], -1e30) for k in each
    ]
    weights = [
        jnp.exp(score - jnp.max(score, axis=-1, keepdims=True)).astype(BF) for score in scores
    ]
    mixed = [dot(weights[k], jnp.concatenate([values[k], ones], axis=1)) for k in each]
    inverse = [1.0 / unstacked(rows[:, width:]) for rows in mixed]
    attn = [unstacked(mixed[k][:, :width]) * inverse[k] for k in each]
    attn = jnp.concatenate(attn, axis=0)
    inverse = jnp.concatenate(inverse, axis=0)
    row_head = lax.broadcasted_iota(jnp.int32, (width, width), 0) // head
    lane_head = lax.broadcasted_iota(jnp.int32, (width, width), 1) // head
    spread = jnp.where(row_head == lane_head, 1.0 / head, 0.0).astype(BF)
    shared = (dot((d_attn * attn).astype(BF), spread) * inverse).astype(BF)
    scaled = (d_attn * inverse).astype(BF)
    g_rows, s_rows = [], []
    for k in each:
        block = slice(k * QUERY_BLOCK, (k + 1) * QUERY_BLOCK)
        g_rows.append(stacked(scaled[block, :]))
        s_rows.append(stacked(shared[block, :]))
    d_probs = [
        dot_nt(
            jnp.concatenate([g_rows[k], s_rows[k]], axis=1),
            jnp.concatenate([values[k], -ones], axis=1),
        )
        for k in each
    ]
    d_scores = [(weights[k].astype(F32) * d_probs[k]).astype(BF) for k in each]
    d_values = [dot_tn(weights[k], g_rows[k]) for k in each]
    d_keys = [dot_tn(d_scores[k], q_rows[k]) for k in each]
    d_query = None
    if wanted:
        d_query = [unstacked(dot(d_scores[k], keys[k])) * scale for k in each]
        d_query = jnp.concatenate(d_query, axis=0).astype(BF)
    for k in each:
        dkeys_s[pl.ds(starts[k], KEY_SPAN), :] += d_keys[k]
        dvalues_s[pl.ds(starts[k], KEY_SPAN), :] += d_values[k]
    return attn, d_query


def main_kernel(
    shift_smem,
    tok_smem,
    tok,
    low_buf,
    high_buf,
    below,
    proj,
    query,
    hidden,
    cot,
    keys,
    values,
    bias_rows,
    pair,
    bias_weight,
    out_weight,
    gain,
    w_query,
    w_key,
    w_value,
    out_ref,
    grad_ref,
    mine_ref,
    other_ref,
    table,
    pair_s,
    keys_s,
    values_s,
    dkeys_s,
    dvalues_s,
    dq_s,
    total_s,
    sems,
):
    atoms, width = hidden.shape
    head = width // HEADS
    groups = atoms // (QUERY_BLOCK * STEP_WINDOWS)
    rows_in = atoms // groups
    count = rows_in // QUERY_BLOCK
    tok_ext = total_s.shape[0] - SPAN
    limit = below.shape[0] + proj.shape[0]
    seq_place, rep_place = lax.axis_index("seq"), lax.axis_index("rep")
    rep = lax.axis_size("rep")
    group_place = seq_place * rep + rep_place
    tok_first = seq_place * proj.shape[0] - (below.shape[0] - RIM)
    tok_low = tok_first - RIM
    core = rep_place % 2
    first = group_place * atoms - RIM
    total = atoms * lax.axis_size("seq") * rep
    cot_at = 2 * RIM_WINDOWS * SUB
    atom_at = cot_at + REACH
    aux_at = atom_at + 2 * SUB

    early = groups - (sems.shape[0] - 2)
    pair_rows = pair.shape[0] // groups
    feats = bias_weight.shape[1]

    def pair_copy(group):
        source = pl.ds(pl.multiple_of(group * pair_rows, pair_rows), pair_rows)
        target = pl.ds(pl.multiple_of((group - early) * pair_rows, pair_rows), pair_rows)
        return pltpu.make_async_copy(
            pair.at[source, :], pair_s.at[target, :], sems.at[group - early + 2]
        )

    own = pl.ds(RIM, atoms)
    key_copy = pltpu.make_async_copy(keys, keys_s.at[own, :], sems.at[0])
    value_copy = pltpu.make_async_copy(values, values_s.at[own, :], sems.at[1])
    key_copy.start()
    value_copy.start()
    for group in range(early, groups):
        pair_copy(group).start()

    dkeys_s[...] = jnp.zeros_like(dkeys_s)
    dvalues_s[...] = jnp.zeros_like(dvalues_s)
    total_s[...] = jnp.zeros_like(total_s)
    fill_table(table, below, proj, high_buf[aux_at + AUX :, :])

    ends = [
        tok_smem[0, 0] - tok_low - RIM,
        tok_smem[tok_smem.shape[0] - 1, SUB - 1] - tok_low,
    ]
    bufs = [low_buf, high_buf]
    ids, bases, atoms_in, shifts = [], [], [], []
    lane = lax.broadcasted_iota(jnp.int32, (1, SUB), 1)
    for buf, end in zip(bufs, ends):
        base = aligned(end, limit)
        offset = ((base + tok_low) & 2047).astype(F32)
        aux = buf[aux_at : aux_at + AUX, :].astype(F32)
        for k in range(2):
            part = aux[k : k + 1, :] * 256.0 + aux[2 + k : 3 + k, :] - offset
            ids.append(jnp.where(part < 0.0, part + 2048.0, part))
            bases.append(base)
        atoms_in.append(buf[atom_at : atom_at + 2 * SUB, :].astype(F32))
        for k in range(RIM_WINDOWS):
            value = jnp.sum(jnp.where(lane == k, aux[4:5, :], 0.0))
            shifts.append(jnp.clip(value.astype(jnp.int32), 0, REACH))
    rim = jnp.concatenate(atoms_in, axis=0)
    rim += jnp.concatenate(token_rows(ids, bases, table), axis=0)
    q_rim, k_rim, v_rim = project(rim, gain, w_query, w_key, w_value)
    skip = 2 * SUB - RIM
    for target, rows in ((keys_s, k_rim), (values_s, v_rim)):
        target[0:RIM, :] = rows[skip : 2 * SUB]
        target[RIM + atoms :, :] = rows[2 * SUB : 2 * SUB + RIM]

    def rim_bias(buf, k):
        at = 2 * k * SUB
        return buf[at : at + SUB, :].astype(F32) + buf[at + SUB : at + 2 * SUB, :].astype(F32)

    starts, q_in, bias = [], [], []
    for side, buf in enumerate(bufs):
        q_at = 2 * SUB if side else 2 * SUB - REACH
        for k in range(RIM_WINDOWS):
            origin = k * QUERY_BLOCK + (REACH + atoms if side else 0)
            starts.append(origin + shifts[side * RIM_WINDOWS + k])
            at = q_at + k * QUERY_BLOCK
            q_in.append(q_rim[at : at + QUERY_BLOCK])
            bias.append(lambda buf=buf, k=k: rim_bias(buf, k))
    cots = [buf[cot_at : cot_at + REACH, :] for buf in bufs]
    grads = dot_nt(jnp.concatenate(cots, axis=0), out_weight[...])
    key_copy.wait()
    value_copy.wait()
    attend(starts, first, total, bias, q_in, grads, keys_s, values_s, dkeys_s, dvalues_s, False)

    def work(group, late):
        rows = pl.ds(pl.multiple_of(group * rows_in, rows_in), rows_in)
        queries = query[rows, :]
        starts, q_in, bias = [], [], []
        for k in range(count):
            window = group * count + k
            starts.append(window * QUERY_BLOCK + REACH + shift_smem[window])
            q_in.append(queries[k * QUERY_BLOCK : (k + 1) * QUERY_BLOCK, :])
            if late:
                at = (group - early) * pair_rows + 2 * k * feats
                at = pl.multiple_of(at, feats)
                bias.append(lambda at=at: pair_bias(pair_s, at, feats, bias_weight[...]))
            else:
                at = pl.multiple_of(window * SUB, SUB)
                bias.append(lambda at=at: bias_rows[pl.ds(at, SUB), :])
        grads = dot_nt(cot[rows, :], out_weight[...])
        attn, d_query = attend(
            starts, first, total, bias, q_in, grads, keys_s, values_s, dkeys_s, dvalues_s, True
        )
        dq_s[rows, :] = d_query
        out_ref[rows, :] = (hidden[rows, :] + dot(attn.astype(BF), out_weight[...])).astype(BF)

    def first_work(group, carry):
        work(group, False)
        return carry

    def later_work(group, carry):
        pair_copy(group).wait()
        work(group, True)
        return carry

    lax.fori_loop(0, early, first_work, 0)
    lax.fori_loop(early, groups, later_work, 0)

    scale = head ** (-0.5)
    chunk = min(1024, atoms)
    blocks = range(chunk // SUB)
    reach = SUB + 16
    row = lax.broadcasted_iota(jnp.int32, (reach, SUB), 0)
    for part in range(atoms // chunk):
        rows = slice(part * chunk, (part + 1) * chunk)
        ext = slice(RIM + part * chunk, RIM + (part + 1) * chunk)
        d_normed = dot_nt(dq_s[rows, :], w_query[...])
        d_normed += dot_nt((dkeys_s[ext, :] * scale).astype(BF), w_key[...])
        d_normed += dot_nt(dvalues_s[ext, :].astype(BF), w_value[...])
        center, inv = centered(hidden[rows, :])
        unit = center * inv
        scaled = d_normed * gain[...]
        d_front = inv * (
            scaled
            - jnp.mean(scaled, axis=-1, keepdims=True)
            - unit * jnp.mean(scaled * unit, axis=-1, keepdims=True)
        )
        grad = (cot[rows, :].astype(F32) + d_front).astype(BF)
        grad_ref[rows, :] = grad
        both = jnp.concatenate([grad, out_ref[rows, :]], axis=1)
        lead = part * len(blocks)
        bases = [aligned(tok_smem[lead + k, 0] - tok_first, tok_ext) for k in blocks]
        ids = [tok[lead + k : lead + k + 1, :] - (tok_first + bases[k]) for k in blocks]
        hot = [jnp.where(row == line, 1.0, 0.0).astype(BF) for line in ids]
        sums = [dot(hot[k], both[k * SUB : (k + 1) * SUB, :]) for k in blocks]
        for k in blocks:
            total_s[pl.ds(bases[k], reach), :] += sums[k]
    quarter = tok_ext // 6
    for target, owner in ((mine_ref, core), (other_ref, 1 - core)):
        for k in range(3):
            at = pl.multiple_of((2 * k + owner) * quarter, quarter)
            target[k * quarter : (k + 1) * quarter, :] = total_s[pl.ds(at, quarter), :].astype(BF)


def body(
    atom_single,
    token_single,
    tok_weight,
    atom_gain,
    w_query,
    w_key,
    w_value,
    pair_weight,
    out_weight,
    pair_feats,
    counts,
    atom_token,
    window_shift,
    atom_cot,
):
    seq = lax.axis_size("seq")
    rep = lax.axis_size("rep")
    rep_place = lax.axis_index("rep")
    atoms, width = atom_single.shape
    tok_rows, tok_width = token_single.shape
    half_rows = tok_rows // 2
    below_rows = half_rows + RIM
    table_rows = below_rows + tok_rows + SPAN
    windows = atoms // QUERY_BLOCK
    channels = pair_feats.shape[1]
    feats = QUERY_BLOCK * channels
    smem = pl.BlockSpec(memory_space=pltpu.SMEM)
    params = pltpu.CompilerParams(vmem_limit_bytes=VMEM)

    tok2 = atom_token.reshape(atoms // SUB, SUB)
    gain = atom_gain.reshape(1, width)
    pair2 = pair_feats.reshape(atoms * channels, KEY_SPAN)
    bias_shape = (BIAS_PARTS * HEADS * HALF, HALF * channels)
    core = rep_place % 2
    proj = dot(token_single, tok_weight).astype(BF)
    below = lax.ppermute(
        proj[tok_rows - below_rows :], "seq", [(i, i + 1) for i in range(seq - 1)]
    )
    up_rows = 2 * RIM_WINDOWS * SUB + REACH + 2 * SUB + AUX
    edge = (RIM_WINDOWS + 1) * feats
    bias_weight, down_buf, up_buf = pl.pallas_call(
        prep_kernel,
        grid=(1,),
        in_specs=[
            smem,
            fixed_block(RIM, width, 0),
            whole(tok2.shape),
            fixed_block(edge, KEY_SPAN, 0),
            fixed_block(edge, KEY_SPAN, windows // (RIM_WINDOWS + 1) - 1),
            fixed_block(SUB, width, 0),
            fixed_block(SUB, width, atoms // SUB - 1),
            fixed_block(2 * SUB, width, 0),
            fixed_block(2 * SUB, width, atoms // (2 * SUB) - 1),
            whole(pair_weight.shape[::-1]),
        ],
        out_specs=[
            whole(bias_shape),
            whole((up_rows + RIM, width)),
            whole((up_rows, width)),
        ],
        out_shape=[
            jax.ShapeDtypeStruct(bias_shape, BF),
            jax.ShapeDtypeStruct((up_rows + RIM, width), BF),
            jax.ShapeDtypeStruct((up_rows, width), BF),
        ],
        compiler_params=pltpu.CompilerParams(vmem_limit_bytes=62 << 20),
        cost_estimate=pl.CostEstimate(
            flops=atoms * width * 256, bytes_accessed=atoms * width * 32, transcendentals=0
        ),
        name="prep",
    )(
        window_shift,
        proj,
        tok2,
        pair2,
        pair2,
        atom_cot,
        atom_cot,
        atom_single,
        atom_single,
        pair_weight.T,
    )

    axes = ("seq", "rep")
    everyone = seq * rep
    low_buf = lax.ppermute(up_buf, axes, [(i, i + 1) for i in range(everyone - 1)])
    high_buf = lax.ppermute(down_buf, axes, [(i + 1, i) for i in range(everyone - 1)])

    vmem = pl.BlockSpec(memory_space=pltpu.VMEM)
    hbm = pl.BlockSpec(memory_space=pltpu.HBM)
    groups = windows // STEP_WINDOWS
    early = groups // 2
    rows_f32 = jax.ShapeDtypeStruct((atoms, width), F32)
    rows_bf = jax.ShapeDtypeStruct((atoms, width), BF)
    bias_f32 = jax.ShapeDtypeStruct((early * STEP_WINDOWS * SUB, KEY_SPAN), F32)
    hidden, query, keys, values, bias_rows = pl.pallas_call(
        front_kernel,
        in_specs=[smem, vmem, hbm, hbm] + [vmem] * 5 + [hbm, hbm],
        out_specs=[vmem] * 5,
        out_shape=[rows_f32, rows_bf, rows_f32, rows_f32, bias_f32],
        scratch_shapes=[
            pltpu.VMEM((table_rows, width), BF),
            pltpu.VMEM(bias_shape, BF),
            pltpu.VMEM((early * STEP_WINDOWS * feats, KEY_SPAN), BF),
            pltpu.SemaphoreType.DMA((early + 3,)),
        ],
        compiler_params=pltpu.CompilerParams(vmem_limit_bytes=40 << 20),
        cost_estimate=pl.CostEstimate(
            flops=atoms * width * 2000000, bytes_accessed=atoms * width * 12800, transcendentals=0
        ),
        name="front",
    )(
        tok2,
        tok2,
        below,
        proj,
        atom_single,
        gain,
        w_query,
        w_key,
        w_value,
        bias_weight,
        pair2,
    )

    tok_ext = half_rows + tok_rows
    sums = jax.ShapeDtypeStruct((tok_ext // 2, 2 * width), BF)
    ext = pltpu.VMEM((atoms + 2 * RIM, width), F32)
    atom_out, atom_grad, mine, other = pl.pallas_call(
        main_kernel,
        in_specs=[smem, smem] + [vmem] * 8 + [pl.BlockSpec(memory_space=pl.ANY)] * 2 + [vmem, hbm] + [vmem] * 6,
        out_specs=[vmem] * 4,
        out_shape=[rows_bf, rows_bf, sums, sums],
        scratch_shapes=[
            pltpu.VMEM((table_rows, width), BF),
            pltpu.VMEM(((groups - early) * STEP_WINDOWS * feats, KEY_SPAN), BF),
            ext,
            ext,
            ext,
            ext,
            pltpu.VMEM((atoms, width), BF),
            pltpu.VMEM((tok_ext + SPAN, 2 * width), F32),
            pltpu.SemaphoreType.DMA((groups - early + 2,)),
        ],
        compiler_params=pltpu.CompilerParams(vmem_limit_bytes=40 << 20),
        name="main",
    )(
        window_shift,
        tok2,
        tok2,
        low_buf,
        high_buf,
        below,
        proj,
        query,
        hidden,
        atom_cot,
        keys,
        values,
        bias_rows,
        pair2,
        bias_weight,
        out_weight,
        gain,
        w_query,
        w_key,
        w_value,
    )

    quarter = tok_ext // 6
    swap = [(i, i ^ 1) for i in range(rep)]
    across = [(i, i ^ 2) for i in range(rep)]
    pair_sum = (mine.astype(F32) + lax.ppermute(other, "rep", swap).astype(F32)).astype(BF)
    low_part, own_part = pair_sum[:quarter], pair_sum[quarter:]
    straight = [(i, i - 1) for i in range(1, seq)]
    crossed = [((s + 1) * rep + r, s * rep + (r ^ 2)) for s in range(seq - 1) for r in range(rep)]
    got_straight = lax.ppermute(low_part, "seq", straight)
    got_crossed = lax.ppermute(low_part, axes, crossed)
    got_own = lax.ppermute(own_part, "rep", across)
    half_sum = own_part.astype(F32) + got_own.astype(F32)
    upper = half_sum[quarter:] + (got_straight.astype(F32) + got_crossed.astype(F32))
    half_sum = jnp.concatenate([half_sum[:quarter], upper], axis=0).astype(BF)
    other_sum = lax.ppermute(half_sum, "rep", swap)
    first = jnp.where(core == 0, half_sum, other_sum)
    second = jnp.where(core == 0, other_sum, half_sum)
    totals = jnp.concatenate(
        [first[:quarter], second[:quarter], first[quarter:], second[quarter:]], axis=0
    )
    token_grad = dot_nt(totals[:, :width], tok_weight).astype(BF)
    token_mean = (totals[:, width:].astype(F32) / counts.astype(F32)[:, None]).astype(BF)
    return (atom_out, token_mean, atom_grad, token_grad)


def solution(mesh):
    return jax.shard_map(
        body,
        mesh=mesh,
        in_specs=(
            P(("seq", "rep"), None),
            P("seq", None),
            P(),
            P(),
            P(),
            P(),
            P(),
            P(),
            P(),
            P(("seq", "rep"), None, None),
            P("seq"),
            P(("seq", "rep")),
            P(("seq", "rep")),
            P(("seq", "rep"), None),
        ),
        out_specs=(
            P(("seq", "rep"), None),
            P("seq", None),
            P(("seq", "rep"), None),
            P("seq", None),
        ),
        check_vma=False,
    )
```

```python
import jax
import jax.numpy as jnp
from jax import lax
from jax.experimental import pallas as pl
from jax.experimental.pallas import tpu as pltpu
from jax.sharding import PartitionSpec as P

HEADS = 4
QUERY_BLOCK = 32
KEY_SPAN = 128
REACH = KEY_SPAN - QUERY_BLOCK
RIM = 2 * REACH
RIM_WINDOWS = REACH // QUERY_BLOCK
HALF = QUERY_BLOCK // 2
SUB = 128
SPAN = 256
AUX = 16
STEP_WINDOWS = 16
BIAS_PARTS = 2
BF = jnp.bfloat16
F32 = jnp.float32
VMEM = 62 << 20


def dot(left, right):
    return jnp.dot(left, right, preferred_element_type=F32)


def dot_nt(left, right):
    return lax.dot_general(left, right, (((1,), (1,)), ((), ())), preferred_element_type=F32)


def dot_tn(left, right):
    return lax.dot_general(left, right, (((0,), (0,)), ((), ())), preferred_element_type=F32)


def whole(shape):
    return pl.BlockSpec(shape, lambda *_: (0,) * len(shape))


def fixed_block(rows, width, index):
    return pl.BlockSpec((rows, width), lambda *_: (index, 0))


def aligned(index, limit):
    return pl.multiple_of(jnp.clip(index, 0, limit - 1) // 16 * 16, 16)


def rows_copy(source, target, at, sem):
    return pltpu.make_async_copy(source, target.at[pl.ds(at, source.shape[0]), :], sem)


def fill_table(table, below, proj, above):
    low, own = below.shape[0], proj.shape[0]
    table[0:low, :] = below[...]
    table[low : low + own, :] = proj[...]
    rest = table.shape[0] - low - own
    high = 0 if above is None else above.shape[0]
    if high:
        table[low + own : low + own + high, :] = above
    table[low + own + high :, :] = jnp.zeros((rest - high, table.shape[1]), BF)


def token_rows(ids, bases, table):
    lane = lax.broadcasted_iota(jnp.int32, (SUB, SPAN), 1).astype(F32)
    ids = [jnp.broadcast_to(row, (SUB, SUB)).T for row in ids]
    hot = [
        jnp.where(jnp.concatenate([row, row], axis=1) == lane, 1.0, 0.0).astype(BF) for row in ids
    ]
    return [dot(one, table[pl.ds(base, SPAN), :]) for one, base in zip(hot, bases)]


def centered(rows):
    center = rows - jnp.mean(rows, axis=-1, keepdims=True)
    spread = jnp.mean(center * center, axis=-1, keepdims=True)
    return center, lax.rsqrt(spread + 1e-05)


def pair_bias(pair, at, feats, bias_weight):
    both = jnp.concatenate(
        [pair[pl.ds(at, feats), :], pair[pl.ds(at + feats, feats), :]], axis=1
    )
    parts = dot(bias_weight, both)
    heads = HEADS * HALF
    parts = parts[:heads] + parts[heads:]
    return jnp.concatenate([parts[:, :KEY_SPAN], parts[:, KEY_SPAN:]], axis=0)


def bias_matrix(pair_weight):
    channels = pair_weight.shape[1]
    heads = HEADS * HALF
    wide = HALF * channels
    pick = lax.broadcasted_iota(jnp.int32, (heads, HEADS), 0) // HALF
    pick = (pick == lax.broadcasted_iota(jnp.int32, (heads, HEADS), 1)).astype(F32).astype(BF)
    copies = lax.broadcasted_iota(jnp.int32, (channels, wide), 1) % channels
    copies = copies == lax.broadcasted_iota(jnp.int32, (channels, wide), 0)
    copies = copies.astype(F32).astype(BF)
    row = lax.broadcasted_iota(jnp.int32, (heads, wide), 0) % HALF
    same = row == lax.broadcasted_iota(jnp.int32, (heads, wide), 1) // channels
    parts = []
    remainder = pair_weight
    for _ in range(BIAS_PARTS):
        upper = remainder.astype(BF)
        remainder = remainder - upper.astype(F32)
        rows = dot(pick, upper).astype(BF)
        parts.append(jnp.where(same, dot(rows, copies), 0.0).astype(BF))
    return jnp.concatenate(parts, axis=0)


def prep_kernel(
    shift_smem,
    proj,
    tok,
    pair_first,
    pair_last,
    cot_first,
    cot_last,
    atom_first,
    atom_last,
    pair_weight,
    bias_out,
    down_out,
    up_out,
):
    bias_weight = bias_matrix(pair_weight[...])
    bias_out[...] = bias_weight
    feats = bias_weight.shape[1]
    blocks = tok.shape[0]
    windows = shift_smem.shape[0]
    rows = pair_first.shape[0] // (2 * feats)
    row = lax.broadcasted_iota(jnp.int32, (AUX, SUB), 0)
    lane = lax.broadcasted_iota(jnp.int32, (AUX, SUB), 1)
    for target, pair, lead, cot, cot_at, atom, block, window in (
        (down_out, pair_first, 0, cot_first, 0, atom_first, 0, 0),
        (
            up_out,
            pair_last,
            rows - RIM_WINDOWS,
            cot_last,
            cot_last.shape[0] - REACH,
            atom_last,
            blocks - 2,
            windows - RIM_WINDOWS,
        ),
    ):
        for k in range(RIM_WINDOWS):
            bias = pair_bias(pair, (lead + k) * 2 * feats, feats, bias_weight)
            upper = bias.astype(BF)
            target[2 * k * SUB : (2 * k + 1) * SUB, :] = upper
            target[(2 * k + 1) * SUB : (2 * k + 2) * SUB, :] = (bias - upper.astype(F32)).astype(BF)
        at = 2 * RIM_WINDOWS * SUB
        target[at : at + REACH, :] = cot[cot_at : cot_at + REACH, :]
        at += REACH
        skip = 0 if block == 0 else 2 * SUB - RIM
        target[at : at + RIM, :] = atom[skip : skip + RIM, :]
        at += RIM
        ids = [tok[block + k : block + k + 1, :] for k in range(2)]
        aux = jnp.zeros((AUX, SUB), F32)
        for k in range(2):
            aux = jnp.where(row == k, ((ids[k] >> 8) & 7).astype(F32), aux)
            aux = jnp.where(row == 2 + k, (ids[k] & 255).astype(F32), aux)
        for k in range(RIM_WINDOWS):
            aux = jnp.where(
                (row == 4) & (lane == k), shift_smem[window + k].astype(F32), aux
            )
        target[at : at + AUX, :] = aux.astype(BF)
    at = down_out.shape[0] - RIM
    down_out[at : at + RIM, :] = proj[...]


def project(hidden, gain, w_query, w_key, w_value):
    center, inv = centered(hidden)
    normed = (center * inv * gain[...]).astype(BF)
    keys = dot(normed, w_key[...]).astype(BF).astype(F32)
    values = dot(normed, w_value[...]).astype(BF).astype(F32)
    return dot(normed, w_query[...]).astype(BF), keys, values


def front_kernel(
    tok_smem,
    tok,
    below,
    proj,
    atom,
    gain,
    w_query,
    w_key,
    w_value,
    bias_weight,
    pair,
    hidden_out,
    query_out,
    keys_out,
    values_out,
    bias_out,
    table,
    weight_s,
    pair_s,
    sems,
):
    atoms = atom.shape[0]
    groups = sems.shape[0] - 3
    pair_rows = pair_s.shape[0] // groups
    copies = [
        rows_copy(below, table, 0, sems.at[groups]),
        rows_copy(proj, table, below.shape[0], sems.at[groups + 1]),
        pltpu.make_async_copy(bias_weight, weight_s, sems.at[groups + 2]),
    ]
    for copy in copies:
        copy.start()

    def pair_copy(group):
        rows = pl.ds(pl.multiple_of(group * pair_rows, pair_rows), pair_rows)
        return pltpu.make_async_copy(pair.at[rows, :], pair_s.at[rows, :], sems.at[group])

    for group in range(groups):
        pair_copy(group).start()
    limit = below.shape[0] + proj.shape[0]
    tok_low = lax.axis_index("seq") * proj.shape[0] - below.shape[0]
    table[limit:, :] = jnp.zeros((table.shape[0] - limit, table.shape[1]), BF)
    for copy in copies[:2]:
        copy.wait()
    chunk = min(1024, atoms)
    blocks = range(chunk // SUB)
    for part in range(atoms // chunk):
        rows = slice(part * chunk, (part + 1) * chunk)
        lead = part * len(blocks)
        bases = [aligned(tok_smem[lead + k, 0] - tok_low, limit) for k in blocks]
        ids = [
            (tok[lead + k : lead + k + 1, :] - (tok_low + bases[k])).astype(F32) for k in blocks
        ]
        hidden = atom[rows, :].astype(F32) + jnp.concatenate(token_rows(ids, bases, table), axis=0)
        hidden_out[rows, :] = hidden
        query_out[rows, :], keys_out[rows, :], values_out[rows, :] = project(
            hidden, gain, w_query, w_key, w_value
        )
    copies[2].wait()
    feats = weight_s.shape[1]
    count = pair_rows // (2 * feats)

    def work(group, carry):
        pair_copy(group).wait()
        for k in range(count):
            window = group * count + k
            at = pl.multiple_of(window * 2 * feats, feats)
            rows = pl.ds(pl.multiple_of(window * SUB, SUB), SUB)
            bias_out[rows, :] = pair_bias(pair_s, at, feats, weight_s[...])
        return carry

    lax.fori_loop(0, groups, work, 0)


def head_lanes(width):
    return lax.broadcasted_iota(jnp.int32, (HALF, width), 1) // (width // HEADS)


def stacked(rows):
    lane = head_lanes(rows.shape[1])
    parts = []
    for half in range(2):
        piece = rows[half * HALF : (half + 1) * HALF, :]
        for h in range(HEADS):
            parts.append(jnp.where(lane == h, piece, jnp.zeros_like(piece)))
    return jnp.concatenate(parts, axis=0)


def unstacked(rows):
    lane = head_lanes(rows.shape[1])
    parts = []
    for half in range(2):
        piece = None
        for h in range(HEADS):
            at = (half * HEADS + h) * HALF
            part = rows[at : at + HALF, :]
            piece = part if piece is None else jnp.where(lane == h, part, piece)
        parts.append(piece)
    return jnp.concatenate(parts, axis=0)


def attend(starts, first, total, bias, query, d_attn, keys_s, values_s, dkeys_s, dvalues_s, wanted):
    width = query[0].shape[1]
    head = width // HEADS
    scale = head ** (-0.5)
    each = range(len(starts))
    key_lane = lax.broadcasted_iota(jnp.int32, (1, KEY_SPAN), 1)
    ones = jnp.ones((KEY_SPAN, KEY_SPAN), BF)
    spots = [key_lane + (first + start) for start in starts]
    inside = [(spot >= 0) & (spot < total) for spot in spots]
    keys = [keys_s[pl.ds(start, KEY_SPAN), :].astype(BF) for start in starts]
    values = [values_s[pl.ds(start, KEY_SPAN), :].astype(BF) for start in starts]
    q_rows = [stacked(rows) for rows in query]
    bias = [make() for make in bias]
    scores = [
        jnp.where(inside[k], dot_nt(q_rows[k], keys[k]) * scale + bias[k], -1e30) for k in each
    ]
    weights = [
        jnp.exp(score - jnp.max(score, axis=-1, keepdims=True)).astype(BF) for score in scores
    ]
    mixed = [dot(weights[k], jnp.concatenate([values[k], ones], axis=1)) for k in each]
    inverse = [1.0 / unstacked(rows[:, width:]) for rows in mixed]
    attn = [unstacked(mixed[k][:, :width]) * inverse[k] for k in each]
    attn = jnp.concatenate(attn, axis=0)
    inverse = jnp.concatenate(inverse, axis=0)
    row_head = lax.broadcasted_iota(jnp.int32, (width, width), 0) // head
    lane_head = lax.broadcasted_iota(jnp.int32, (width, width), 1) // head
    spread = jnp.where(row_head == lane_head, 1.0 / head, 0.0).astype(BF)
    shared = (dot((d_attn * attn).astype(BF), spread) * inverse).astype(BF)
    scaled = (d_attn * inverse).astype(BF)
    g_rows, s_rows = [], []
    for k in each:
        block = slice(k * QUERY_BLOCK, (k + 1) * QUERY_BLOCK)
        g_rows.append(stacked(scaled[block, :]))
        s_rows.append(stacked(shared[block, :]))
    d_probs = [
        dot_nt(
            jnp.concatenate([g_rows[k], s_rows[k]], axis=1),
            jnp.concatenate([values[k], -ones], axis=1),
        )
        for k in each
    ]
    d_scores = [(weights[k].astype(F32) * d_probs[k]).astype(BF) for k in each]
    d_values = [dot_tn(weights[k], g_rows[k]) for k in each]
    d_keys = [dot_tn(d_scores[k], q_rows[k]) for k in each]
    d_query = None
    if wanted:
        d_query = [unstacked(dot(d_scores[k], keys[k])) * scale for k in each]
        d_query = jnp.concatenate(d_query, axis=0).astype(BF)
    for k in each:
        dkeys_s[pl.ds(starts[k], KEY_SPAN), :] += d_keys[k]
        dvalues_s[pl.ds(starts[k], KEY_SPAN), :] += d_values[k]
    return attn, d_query


def main_kernel(
    shift_smem,
    tok_smem,
    tok,
    low_buf,
    high_buf,
    below,
    proj,
    query,
    hidden,
    cot,
    keys,
    values,
    bias_rows,
    pair,
    bias_weight,
    out_weight,
    gain,
    w_query,
    w_key,
    w_value,
    out_ref,
    grad_ref,
    mine_ref,
    other_ref,
    table,
    pair_s,
    keys_s,
    values_s,
    dkeys_s,
    dvalues_s,
    dq_s,
    total_s,
    sems,
):
    atoms, width = hidden.shape
    head = width // HEADS
    groups = atoms // (QUERY_BLOCK * STEP_WINDOWS)
    rows_in = atoms // groups
    count = rows_in // QUERY_BLOCK
    tok_ext = total_s.shape[0] - SPAN
    limit = below.shape[0] + proj.shape[0]
    seq_place, rep_place = lax.axis_index("seq"), lax.axis_index("rep")
    rep = lax.axis_size("rep")
    group_place = seq_place * rep + rep_place
    tok_first = seq_place * proj.shape[0] - (below.shape[0] - RIM)
    tok_low = tok_first - RIM
    core = rep_place % 2
    first = group_place * atoms - RIM
    total = atoms * lax.axis_size("seq") * rep
    cot_at = 2 * RIM_WINDOWS * SUB
    atom_at = cot_at + REACH
    aux_at = atom_at + RIM

    early = groups - (sems.shape[0] - 2)
    pair_rows = pair.shape[0] // groups
    feats = bias_weight.shape[1]

    def pair_copy(group):
        source = pl.ds(pl.multiple_of(group * pair_rows, pair_rows), pair_rows)
        target = pl.ds(pl.multiple_of((group - early) * pair_rows, pair_rows), pair_rows)
        return pltpu.make_async_copy(
            pair.at[source, :], pair_s.at[target, :], sems.at[group - early + 2]
        )

    own = pl.ds(RIM, atoms)
    key_copy = pltpu.make_async_copy(keys, keys_s.at[own, :], sems.at[0])
    value_copy = pltpu.make_async_copy(values, values_s.at[own, :], sems.at[1])
    key_copy.start()
    value_copy.start()
    for group in range(early, groups):
        pair_copy(group).start()

    dkeys_s[...] = jnp.zeros_like(dkeys_s)
    dvalues_s[...] = jnp.zeros_like(dvalues_s)
    total_s[...] = jnp.zeros_like(total_s)
    fill_table(table, below, proj, high_buf[aux_at + AUX :, :])

    ends = [
        tok_smem[0, 0] - tok_low - RIM,
        tok_smem[tok_smem.shape[0] - 1, SUB - 1] - tok_low,
    ]
    bufs = [low_buf, high_buf]
    ids, bases, atoms_in, shifts = [], [], [], []
    lane = lax.broadcasted_iota(jnp.int32, (1, SUB), 1)
    for buf, end in zip(bufs, ends):
        base = aligned(end, limit)
        offset = ((base + tok_low) & 2047).astype(F32)
        aux = buf[aux_at : aux_at + AUX, :].astype(F32)
        for k in range(2):
            part = aux[k : k + 1, :] * 256.0 + aux[2 + k : 3 + k, :] - offset
            ids.append(jnp.where(part < 0.0, part + 2048.0, part))
            bases.append(base)
        atoms_in.append(buf[atom_at : atom_at + RIM, :].astype(F32))
        for k in range(RIM_WINDOWS):
            value = jnp.sum(jnp.where(lane == k, aux[4:5, :], 0.0))
            shifts.append(jnp.clip(value.astype(jnp.int32), 0, REACH))
    gap = jnp.zeros((2 * SUB - RIM, width), F32)
    rim = jnp.concatenate([gap, atoms_in[0], atoms_in[1], gap], axis=0)
    rim += jnp.concatenate(token_rows(ids, bases, table), axis=0)
    q_rim, k_rim, v_rim = project(rim, gain, w_query, w_key, w_value)
    skip = 2 * SUB - RIM
    for target, rows in ((keys_s, k_rim), (values_s, v_rim)):
        target[0:RIM, :] = rows[skip : 2 * SUB]
        target[RIM + atoms :, :] = rows[2 * SUB : 2 * SUB + RIM]

    def rim_bias(buf, k):
        at = 2 * k * SUB
        return buf[at : at + SUB, :].astype(F32) + buf[at + SUB : at + 2 * SUB, :].astype(F32)

    starts, q_in, bias = [], [], []
    for side, buf in enumerate(bufs):
        q_at = 2 * SUB if side else 2 * SUB - REACH
        for k in range(RIM_WINDOWS):
            origin = k * QUERY_BLOCK + (REACH + atoms if side else 0)
            starts.append(origin + shifts[side * RIM_WINDOWS + k])
            at = q_at + k * QUERY_BLOCK
            q_in.append(q_rim[at : at + QUERY_BLOCK])
            bias.append(lambda buf=buf, k=k: rim_bias(buf, k))
    cots = [buf[cot_at : cot_at + REACH, :] for buf in bufs]
    grads = dot_nt(jnp.concatenate(cots, axis=0), out_weight[...])
    key_copy.wait()
    value_copy.wait()
    attend(starts, first, total, bias, q_in, grads, keys_s, values_s, dkeys_s, dvalues_s, False)

    def work(group, late):
        rows = pl.ds(pl.multiple_of(group * rows_in, rows_in), rows_in)
        queries = query[rows, :]
        starts, q_in, bias = [], [], []
        for k in range(count):
            window = group * count + k
            starts.append(window * QUERY_BLOCK + REACH + shift_smem[window])
            q_in.append(queries[k * QUERY_BLOCK : (k + 1) * QUERY_BLOCK, :])
            if late:
                at = (group - early) * pair_rows + 2 * k * feats
                at = pl.multiple_of(at, feats)
                bias.append(lambda at=at: pair_bias(pair_s, at, feats, bias_weight[...]))
            else:
                at = pl.multiple_of(window * SUB, SUB)
                bias.append(lambda at=at: bias_rows[pl.ds(at, SUB), :])
        grads = dot_nt(cot[rows, :], out_weight[...])
        attn, d_query = attend(
            starts, first, total, bias, q_in, grads, keys_s, values_s, dkeys_s, dvalues_s, True
        )
        dq_s[rows, :] = d_query
        out_ref[rows, :] = (hidden[rows, :] + dot(attn.astype(BF), out_weight[...])).astype(BF)

    def first_work(group, carry):
        work(group, False)
        return carry

    def later_work(group, carry):
        pair_copy(group).wait()
        work(group, True)
        return carry

    lax.fori_loop(0, early, first_work, 0)
    lax.fori_loop(early, groups, later_work, 0)

    scale = head ** (-0.5)
    chunk = min(1024, atoms)
    blocks = range(chunk // SUB)
    reach = SUB + 16
    row = lax.broadcasted_iota(jnp.int32, (reach, SUB), 0)
    for part in range(atoms // chunk):
        rows = slice(part * chunk, (part + 1) * chunk)
        ext = slice(RIM + part * chunk, RIM + (part + 1) * chunk)
        d_normed = dot_nt(dq_s[rows, :], w_query[...])
        d_normed += dot_nt((dkeys_s[ext, :] * scale).astype(BF), w_key[...])
        d_normed += dot_nt(dvalues_s[ext, :].astype(BF), w_value[...])
        center, inv = centered(hidden[rows, :])
        unit = center * inv
        scaled = d_normed * gain[...]
        d_front = inv * (
            scaled
            - jnp.mean(scaled, axis=-1, keepdims=True)
            - unit * jnp.mean(scaled * unit, axis=-1, keepdims=True)
        )
        grad = (cot[rows, :].astype(F32) + d_front).astype(BF)
        grad_ref[rows, :] = grad
        both = jnp.concatenate([grad, out_ref[rows, :]], axis=1)
        lead = part * len(blocks)
        bases = [aligned(tok_smem[lead + k, 0] - tok_first, tok_ext) for k in blocks]
        ids = [tok[lead + k : lead + k + 1, :] - (tok_first + bases[k]) for k in blocks]
        hot = [jnp.where(row == line, 1.0, 0.0).astype(BF) for line in ids]
        sums = [dot(hot[k], both[k * SUB : (k + 1) * SUB, :]) for k in blocks]
        for k in blocks:
            total_s[pl.ds(bases[k], reach), :] += sums[k]
    quarter = tok_ext // 6
    for target, owner in ((mine_ref, core), (other_ref, 1 - core)):
        for k in range(3):
            at = pl.multiple_of((2 * k + owner) * quarter, quarter)
            target[k * quarter : (k + 1) * quarter, :] = total_s[pl.ds(at, quarter), :].astype(BF)


def body(
    atom_single,
    token_single,
    tok_weight,
    atom_gain,
    w_query,
    w_key,
    w_value,
    pair_weight,
    out_weight,
    pair_feats,
    counts,
    atom_token,
    window_shift,
    atom_cot,
):
    seq = lax.axis_size("seq")
    rep = lax.axis_size("rep")
    rep_place = lax.axis_index("rep")
    atoms, width = atom_single.shape
    tok_rows, tok_width = token_single.shape
    half_rows = tok_rows // 2
    below_rows = half_rows + RIM
    table_rows = below_rows + tok_rows + SPAN
    windows = atoms // QUERY_BLOCK
    channels = pair_feats.shape[1]
    feats = QUERY_BLOCK * channels
    smem = pl.BlockSpec(memory_space=pltpu.SMEM)
    params = pltpu.CompilerParams(vmem_limit_bytes=VMEM)

    tok2 = atom_token.reshape(atoms // SUB, SUB)
    gain = atom_gain.reshape(1, width)
    pair2 = pair_feats.reshape(atoms * channels, KEY_SPAN)
    bias_shape = (BIAS_PARTS * HEADS * HALF, HALF * channels)
    core = rep_place % 2
    proj = dot(token_single, tok_weight).astype(BF)
    below = lax.ppermute(
        proj[tok_rows - below_rows :], "seq", [(i, i + 1) for i in range(seq - 1)]
    )
    up_rows = 2 * RIM_WINDOWS * SUB + REACH + RIM + AUX
    edge = (RIM_WINDOWS + 1) * feats
    bias_weight, down_buf, up_buf = pl.pallas_call(
        prep_kernel,
        grid=(1,),
        in_specs=[
            smem,
            fixed_block(RIM, width, 0),
            whole(tok2.shape),
            fixed_block(edge, KEY_SPAN, 0),
            fixed_block(edge, KEY_SPAN, windows // (RIM_WINDOWS + 1) - 1),
            fixed_block(SUB, width, 0),
            fixed_block(SUB, width, atoms // SUB - 1),
            fixed_block(2 * SUB, width, 0),
            fixed_block(2 * SUB, width, atoms // (2 * SUB) - 1),
            whole(pair_weight.shape[::-1]),
        ],
        out_specs=[
            whole(bias_shape),
            whole((up_rows + RIM, width)),
            whole((up_rows, width)),
        ],
        out_shape=[
            jax.ShapeDtypeStruct(bias_shape, BF),
            jax.ShapeDtypeStruct((up_rows + RIM, width), BF),
            jax.ShapeDtypeStruct((up_rows, width), BF),
        ],
        compiler_params=pltpu.CompilerParams(vmem_limit_bytes=60 << 20),
        cost_estimate=pl.CostEstimate(
            flops=atoms * width * 256, bytes_accessed=atoms * width * 32, transcendentals=0
        ),
        name="prep",
    )(
        window_shift,
        proj,
        tok2,
        pair2,
        pair2,
        atom_cot,
        atom_cot,
        atom_single,
        atom_single,
        pair_weight.T,
    )

    axes = ("seq", "rep")
    everyone = seq * rep
    low_buf = lax.ppermute(up_buf, axes, [(i, i + 1) for i in range(everyone - 1)])
    high_buf = lax.ppermute(down_buf, axes, [(i + 1, i) for i in range(everyone - 1)])

    vmem = pl.BlockSpec(memory_space=pltpu.VMEM)
    hbm = pl.BlockSpec(memory_space=pltpu.HBM)
    groups = windows // STEP_WINDOWS
    early = groups - 1
    rows_f32 = jax.ShapeDtypeStruct((atoms, width), F32)
    rows_bf = jax.ShapeDtypeStruct((atoms, width), BF)
    bias_f32 = jax.ShapeDtypeStruct((early * STEP_WINDOWS * SUB, KEY_SPAN), F32)
    hidden, query, keys, values, bias_rows = pl.pallas_call(
        front_kernel,
        in_specs=[smem, vmem, hbm, hbm] + [vmem] * 5 + [hbm, hbm],
        out_specs=[vmem] * 5,
        out_shape=[rows_f32, rows_bf, rows_f32, rows_f32, bias_f32],
        scratch_shapes=[
            pltpu.VMEM((table_rows, width), BF),
            pltpu.VMEM(bias_shape, BF),
            pltpu.VMEM((early * STEP_WINDOWS * feats, KEY_SPAN), BF),
            pltpu.SemaphoreType.DMA((early + 3,)),
        ],
        compiler_params=pltpu.CompilerParams(vmem_limit_bytes=40 << 20),
        cost_estimate=pl.CostEstimate(
            flops=atoms * width * 2000000, bytes_accessed=atoms * width * 12800, transcendentals=0
        ),
        name="front",
    )(
        tok2,
        tok2,
        below,
        proj,
        atom_single,
        gain,
        w_query,
        w_key,
        w_value,
        bias_weight,
        pair2,
    )

    tok_ext = half_rows + tok_rows
    sums = jax.ShapeDtypeStruct((tok_ext // 2, 2 * width), BF)
    ext = pltpu.VMEM((atoms + 2 * RIM, width), F32)
    atom_out, atom_grad, mine, other = pl.pallas_call(
        main_kernel,
        in_specs=[smem, smem] + [vmem] * 8 + [pl.BlockSpec(memory_space=pl.ANY)] * 2 + [vmem, hbm] + [vmem] * 6,
        out_specs=[vmem] * 4,
        out_shape=[rows_bf, rows_bf, sums, sums],
        scratch_shapes=[
            pltpu.VMEM((table_rows, width), BF),
            pltpu.VMEM(((groups - early) * STEP_WINDOWS * feats, KEY_SPAN), BF),
            ext,
            ext,
            ext,
            ext,
            pltpu.VMEM((atoms, width), BF),
            pltpu.VMEM((tok_ext + SPAN, 2 * width), F32),
            pltpu.SemaphoreType.DMA((groups - early + 2,)),
        ],
        compiler_params=pltpu.CompilerParams(vmem_limit_bytes=40 << 20),
        name="main",
    )(
        window_shift,
        tok2,
        tok2,
        low_buf,
        high_buf,
        below,
        proj,
        query,
        hidden,
        atom_cot,
        keys,
        values,
        bias_rows,
        pair2,
        bias_weight,
        out_weight,
        gain,
        w_query,
        w_key,
        w_value,
    )

    quarter = tok_ext // 6
    swap = [(i, i ^ 1) for i in range(rep)]
    across = [(i, i ^ 2) for i in range(rep)]
    pair_sum = (mine.astype(F32) + lax.ppermute(other, "rep", swap).astype(F32)).astype(BF)
    low_part, own_part = pair_sum[:quarter], pair_sum[quarter:]
    straight = [(i, i - 1) for i in range(1, seq)]
    crossed = [((s + 1) * rep + r, s * rep + (r ^ 2)) for s in range(seq - 1) for r in range(rep)]
    got_straight = lax.ppermute(low_part, "seq", straight)
    got_crossed = lax.ppermute(low_part, axes, crossed)
    got_own = lax.ppermute(own_part, "rep", across)
    half_sum = own_part.astype(F32) + got_own.astype(F32)
    upper = half_sum[quarter:] + (got_straight.astype(F32) + got_crossed.astype(F32))
    half_sum = jnp.concatenate([half_sum[:quarter], upper], axis=0).astype(BF)
    other_sum = lax.ppermute(half_sum, "rep", swap)
    first = jnp.where(core == 0, half_sum, other_sum)
    second = jnp.where(core == 0, other_sum, half_sum)
    totals = jnp.concatenate(
        [first[:quarter], second[:quarter], first[quarter:], second[quarter:]], axis=0
    )
    token_grad = dot_nt(totals[:, :width], tok_weight).astype(BF)
    token_mean = (totals[:, width:].astype(F32) / counts.astype(F32)[:, None]).astype(BF)
    return (atom_out, token_mean, atom_grad, token_grad)


def solution(mesh):
    return jax.shard_map(
        body,
        mesh=mesh,
        in_specs=(
            P(("seq", "rep"), None),
            P("seq", None),
            P(),
            P(),
            P(),
            P(),
            P(),
            P(),
            P(),
            P(("seq", "rep"), None, None),
            P("seq"),
            P(("seq", "rep")),
            P(("seq", "rep")),
            P(("seq", "rep"), None),
        ),
        out_specs=(
            P(("seq", "rep"), None),
            P("seq", None),
            P(("seq", "rep"), None),
            P("seq", None),
        ),
        check_vma=False,
    )
```
